256 devices in a mesh: seq: 128 (over x_hi, z, y, core), tp: 2 (over x_lo).
Axes of the slice: x: 4 (x_hi: 2, x_lo: 2; x = x_hi * 2 + x_lo), y: 4, z: 8, core: 2. Of those that a mesh axis runs over, the one named last changes fastest.
Arguments:
- residual_in: bfloat16 [32768, 1024], P('seq', 'tp'), may hold values from -6 to 6
- queries: bfloat16 [32768, 1024], P('seq', 'tp'), may hold values from -240 to 240
- keys: bfloat16 [32768, 1024], P('seq', 'tp'), may hold values from -12 to 12
- values: bfloat16 [32768, 1024], P('seq', 'tp'), may hold values from -6 to 6
- head_offset: int32 [6, 16], P(None, 'tp'), may hold values from 0 to 31
- out_weight: bfloat16 [1024, 1024], P('tp'), may hold values from -0.1875 to 0.1875
- norm_gain: float32 [1024], replicated, may hold values from 0.5 to 1.5
- gate_weight: bfloat16 [1024, 2048], P(None, 'tp'), may hold values from -0.1875 to 0.1875
- up_weight: bfloat16 [1024, 2048], P(None, 'tp'), may hold values from -0.1875 to 0.1875
- down_weight: bfloat16 [2048, 1024], P('tp'), may hold values from -0.125 to 0.125
Outputs:
- layer_out: bfloat16 [32768, 1024], P('seq', 'tp')
The draws below stay inside these ranges and needn't reach their ends.
All inputs are finite; a program needn't handle non-finite values.
Results may differ from the reference program's by a relative error of at most 0.0095.
Values may be sent and summed in bfloat16 or wider, within the bound.
A program may use at most 128 MiB of HBM per device.

```python
import math
import jax
import jax.numpy as jnp
from jax import lax

D = 1024
HEADS = 16
HEAD_DIM = 64
FF = 2048
BRANCHES = 6
TOK_DEV = 256
TOKENS = 32768
WIDEST = 16384


def shared_keys(key):
    return jnp.clip(jax.random.normal(key, (TOKENS, D), jnp.float32), -6.0, 6.0)


def draw_keys(key, part):
    base = shared_keys(key)
    return base.astype(jnp.bfloat16)


def draw_queries(key, part):
    key = jax.random.fold_in(key, 5)
    return jnp.clip(2.0 * jax.random.normal(key, (TOKENS, D), jnp.float32), -12.0, 12.0).astype(jnp.bfloat16)


def place_ends(values, rng, low, top_value):
    shape = values.shape
    spot = [jax.random.randint(jax.random.fold_in(rng, axis), (), 0, shape[axis]) for axis in range(len(shape))]
    values = values.at[tuple(spot)].set(low)
    longest = shape.index(max(shape))
    spot[longest] = (spot[longest] + 1) % shape[longest]
    return values.at[tuple(spot)].set(top_value)


def levels(stream_key, dims, shards, smallest, high):
    factor_of, own = 1.0, jax.random.fold_in(stream_key, 6)
    for axis_at, blocks in shards:
        draws = jnp.exp(jax.random.uniform(jax.random.fold_in(own, axis_at), (blocks,), jnp.float32, smallest / len(shards), high / len(shards)))
        factor_of = factor_of * jnp.repeat(draws, dims[axis_at] // blocks).reshape([-1 if axis == axis_at else 1 for axis in range(len(dims))])
    return factor_of


def gaussian(stream_key, extent, deviation, most, cuts=(), kind=jnp.bfloat16):
    values = jax.random.normal(stream_key, extent, jnp.float32) * deviation
    if len(cuts) > 0:
        values = levels(stream_key, extent, cuts, -0.22, 0.18) * values
    return jnp.clip(values, min=-most, max=most).astype(kind)


def setup_inputs(seed: int = 0) -> dict:
    seeds = jax.random.split(jax.random.key(seed), 11)
    residual_in = gaussian(seeds[0], (TOKENS, D), 1.0, 6.0, ((0, 128), (1, 2)))
    queries = draw_queries(jax.random.fold_in(seeds[10], 71), 0)
    keys = draw_keys(jax.random.fold_in(seeds[10], 71), 0)
    values = gaussian(seeds[3], (TOKENS, D), 1.0, 6.0, ((0, 128), (1, 2)))
    head_offset = place_ends(jax.random.randint(seeds[4], (BRANCHES, HEADS), 0, 2 ** (BRANCHES - 1)), jax.random.fold_in(seeds[4], 1), 0, (2 ** (BRANCHES - 1)) - 1).astype(jnp.int32)
    out_weight = gaussian(seeds[5], (D, D), D ** -0.5, 0.1875, ((0, 2),))
    norm_gain = jnp.clip(jax.random.uniform(seeds[6], (D,), jnp.float32, 0.5, 1.5), 0.5, 1.5)
    gate_weight = gaussian(seeds[7], (D, FF), D ** -0.5, 0.1875, ((1, 2),))
    up_weight = gaussian(seeds[8], (D, FF), D ** -0.5, 0.1875, ((1, 2),))
    down_weight = gaussian(seeds[9], (FF, D), FF ** -0.5, 0.125, ((0, 2),))
    return {"residual_in": residual_in, "queries": queries, "keys": keys, "values": values, "head_offset": head_offset, "out_weight": out_weight, "norm_gain": norm_gain, "gate_weight": gate_weight, "up_weight": up_weight, "down_weight": down_weight}


masked_score = -1e+30

def pick_rows(array, choose, rate):
    count = array.shape[0] // rate
    shaped = array.reshape(count, rate, array.shape[1], array.shape[2])
    return lax.optimization_barrier(jnp.sum(shaped * choose[None, :, :, None].astype(array.dtype), axis=1))

def reference(residual_in, queries, keys, values, head_offset, out_weight, norm_gain, gate_weight, up_weight, down_weight):
    query_heads = queries.reshape(TOKENS, HEADS, HEAD_DIM)
    key_heads = keys.reshape(TOKENS, HEADS, HEAD_DIM)
    value_heads = values.reshape(TOKENS, HEADS, HEAD_DIM)
    scale = 1.0 / math.sqrt(HEAD_DIM)
    peak = None
    total = None
    accum = None
    for branch in range(BRANCHES):
        rate = 2 ** branch
        length = min(TOK_DEV * 2 ** (branch + 1), WIDEST)
        segments = TOKENS // length
        inner = length // rate
        offsets = head_offset[branch] % rate
        choose = jnp.arange(rate, dtype=jnp.int32)[:, None] == offsets[None, :]
        picked_query = pick_rows(query_heads, choose, rate).reshape(segments, inner, HEADS, HEAD_DIM)
        picked_key = pick_rows(key_heads, choose, rate).reshape(segments, inner, HEADS, HEAD_DIM)
        picked_value = pick_rows(value_heads, choose, rate).reshape(segments, inner, HEADS, HEAD_DIM)
        causal = jnp.arange(inner, dtype=jnp.int32)[None, :] <= jnp.arange(inner, dtype=jnp.int32)[:, None]

        def attend(block):
            query, key_rows, value_rows = block
            scores = jnp.einsum('qhd,khd->hqk', query.astype(jnp.float32), key_rows.astype(jnp.float32)) * scale
            scores = jnp.where(causal[None], scores, masked_score)
            top = lax.optimization_barrier(jnp.max(scores, axis=2, keepdims=True))
            log_total = top + jnp.log(lax.optimization_barrier(jnp.sum(jnp.exp(scores - top), axis=2, keepdims=True)))
            weights = jnp.exp(scores - log_total).astype(jnp.bfloat16)
            output = jnp.einsum('hqk,khd->qhd', weights.astype(jnp.float32), value_rows.astype(jnp.float32))
            return (output, jnp.transpose(log_total[:, :, 0]))
        outputs, logs = lax.map(attend, (picked_query, picked_key, picked_value))
        chosen = choose.astype(jnp.float32)
        count = TOKENS // rate
        spread = (outputs.reshape(count, 1, HEADS, HEAD_DIM) * chosen[None, :, :, None]).reshape(TOKENS, HEADS, HEAD_DIM)
        spread_log = jnp.broadcast_to(logs.reshape(count, 1, HEADS), (count, rate, HEADS)).reshape(TOKENS, HEADS)
        covered = jnp.broadcast_to(choose[None], (count, rate, HEADS)).reshape(TOKENS, HEADS)
        if branch == 0:
            peak = spread_log
            total = jnp.ones((TOKENS, HEADS), jnp.float32)
            accum = spread
        else:
            new_peak = jnp.where(covered, jnp.maximum(peak, spread_log), peak)
            keep = jnp.exp(peak - new_peak)
            branch_weight = jnp.where(covered, jnp.exp(jnp.where(covered, spread_log, new_peak) - new_peak), 0.0)
            total = total * keep + branch_weight
            accum = accum * keep[..., None] + branch_weight[..., None] * spread
            peak = new_peak
    mix = (accum / total[..., None]).astype(jnp.bfloat16).reshape(TOKENS, D)
    hidden = residual_in.astype(jnp.float32) + jnp.dot(mix, out_weight, preferred_element_type=jnp.float32)
    inverse = lax.rsqrt(lax.optimization_barrier(jnp.mean(hidden * hidden, axis=1, keepdims=True)) + 1e-05)
    normed = (hidden * inverse * norm_gain[None, :]).astype(jnp.bfloat16)
    gate = jnp.dot(normed, gate_weight, preferred_element_type=jnp.float32)
    up = jnp.dot(normed, up_weight, preferred_element_type=jnp.float32)
    act = (jax.nn.silu(gate) * up).astype(jnp.bfloat16)
    return (hidden + jnp.dot(act, down_weight, preferred_element_type=jnp.float32)).astype(jnp.bfloat16)
```

```python
import math

import jax
import jax.numpy as jnp
from jax import lax
from jax.experimental import pallas as pl
from jax.experimental.pallas import tpu as pltpu
from jax.sharding import PartitionSpec as P

MESH = pl.DeviceIdType.MESH
F32 = jnp.float32
BF16 = jnp.bfloat16

ROWS = 256
COLS = 512
GROUP = 8
ZED = 8
MASKED = -1e30
EXPONENT = math.log2(math.e) / 8.0


def lanes(shape):
    return lax.broadcasted_iota(jnp.int32, shape, len(shape) - 1)


def sublanes(shape):
    return lax.broadcasted_iota(jnp.int32, shape, 0)


def swap(x):
    return pltpu.roll(x, 64, 1)


def mm(a, b):
    return lax.dot_general(a, b, (((1,), (0,)), ((), ())), preferred_element_type=F32)


def mmt(a, b):
    return lax.dot_general(a, b, (((1,), (1,)), ((), ())), preferred_element_type=F32)


def with_ones(kv):
    lane = lanes(kv.shape)
    return jnp.where(lane < 64, jnp.where(lane == 0, 1.0, 0.0), kv.astype(F32)).astype(BF16)


def branch_of(i):
    one = jnp.where(i < 192, 2, jnp.where(i < 224, 3, jnp.where(i < 240, 4, jnp.where(i < 248, 5, 6))))
    return jnp.where(i < 128, 1, one)


def layer(
    queries,
    keys,
    values,
    residual,
    out_weight,
    gain,
    offsets,
    gate_hbm,
    up_hbm,
    down_hbm,
    out,
    send,
    got,
    pick_kv,
    pick_v1,
    pick_q,
    far_q,
    k3,
    k4,
    k5,
    near_out,
    pick_out,
    choose,
    choose_t,
    mix_send,
    mix_own,
    mix_far,
    mix_wide,
    res_all,
    out_far,
    gate_w,
    up_w,
    down_w,
    hidden,
    normed,
    act,
    down_send,
    down_got,
    a_send,
    a_got,
    z_send,
    z_got,
    m_send,
    m_got,
    f_send,
    f_got,
    w_send,
    w_got,
    r_send,
    r_got,
    d_send,
    d_got,
    local,
):
    seq = lax.axis_index("seq")
    tp = lax.axis_index("tp")
    base = (seq // GROUP) * GROUP
    me = seq % GROUP
    y = me // 2
    core = me % 2
    z = (seq // GROUP) % ZED
    half = seq // (GROUP * ZED)
    plane = half * (GROUP * ZED)
    partner = (seq, 1 - tp)
    behind = ((1 - half) * (GROUP * ZED) + seq % (GROUP * ZED), 1 - tp)
    sibling = (base + me + 1 - 2 * core, tp)

    def remote(src, dst, s, r, to):
        return pltpu.make_async_remote_copy(
            src_ref=src, dst_ref=dst, send_sem=s, recv_sem=r, device_id=to, device_id_type=MESH
        )

    loads = [
        pltpu.make_async_copy(gate_hbm, gate_w, local.at[0]),
        pltpu.make_async_copy(up_hbm, up_w, local.at[1]),
        pltpu.make_async_copy(down_hbm, down_w, local.at[2]),
    ]

    k3[...] = jnp.zeros_like(k3)
    k4[...] = jnp.zeros_like(k4)
    k5[...] = jnp.zeros_like(k5)
    barrier = pltpu.get_barrier_semaphore()
    for k in range(1, GROUP):
        pl.semaphore_signal(barrier, inc=1, device_id=(base + (me + k) % GROUP, tp), device_id_type=MESH)
    for d in range(1, ZED):
        pl.semaphore_signal(
            barrier, inc=1, device_id=(plane + ((z + d) % ZED) * GROUP + me, tp), device_id_type=MESH
        )
    pl.semaphore_signal(barrier, inc=1, device_id=partner, device_id_type=MESH)
    pl.semaphore_signal(barrier, inc=1, device_id=behind, device_id_type=MESH)

    low = lanes((ROWS, 128)) < 64
    low_half = lanes((128, 128)) < 64
    for pair in range(GROUP // 2):
        cut = slice(128 * pair, 128 * pair + 128)
        k = keys[:, cut].astype(F32)
        v = values[:, cut].astype(F32)
        q = queries[:, cut].astype(F32)
        send[2 * pair, 0:ROWS] = jnp.where(low, k, swap(v)).astype(BF16)
        send[2 * pair + 1, 0:ROWS] = jnp.where(low, swap(k), v).astype(BF16)
        top, bottom = q[0:128], q[128:256]
        send[2 * pair, ROWS : ROWS + 128] = jnp.where(low_half, top, swap(bottom)).astype(BF16)
        send[2 * pair + 1, ROWS : ROWS + 128] = jnp.where(low_half, swap(top), bottom).astype(BF16)

    pl.semaphore_wait(barrier, 2 * (GROUP - 1) + 2)

    def block_copy(to):
        return remote(send.at[to], got.at[me], a_send.at[to], a_got.at[me], (base + to, tp))

    a_out = []
    for step in (2, 1, 3):
        for c in range(2):
            a_out.append(block_copy(((y + step) % 4) * 2 + c))
            a_out[-1].start()
    a_out.append(block_copy(me + 1 - 2 * core))
    a_out[-1].start()
    got[me] = send[me]

    w_first = core * 128
    w_second = 256 + core * 128

    def w_piece(first, i, to, src):
        piece = pl.ds(pl.multiple_of(first, 128), 128)
        return remote(src.at[piece], out_far.at[piece], w_send.at[i], w_got.at[i], to)

    w_out = [w_piece(w_first, 0, partner, out_weight), w_piece(w_second, 1, behind, out_weight)]
    res_copy = remote(residual, res_all.at[tp], r_send, r_got, partner)
    res_copy.start()
    for copy in w_out:
        copy.start()
    for load in loads:
        load.start()
    res_all[tp] = residual[...]

    def target(i):
        spot = jnp.full(i.shape, -1, jnp.int32)
        first = 0
        for b in range(1, 6):
            rate = 2**b
            count = ROWS // rate
            off = offsets[b, me] & (rate - 1)
            inside = (i >= first) & (i < first + count)
            spot = jnp.where(inside, (i - first) * rate + off, spot)
            first += count
        return spot

    square = (ROWS, ROWS)
    choose[...] = jnp.where(lanes(square) == target(sublanes(square)), 1.0, 0.0).astype(BF16)
    choose_t[...] = jnp.where(sublanes(square) == target(lanes(square)), 1.0, 0.0).astype(BF16)
    pick_out[:, 248:256] = jnp.zeros((GROUP, 8, 128), F32)

    z3 = z % 2
    z4 = z % 4

    def z_copy(which, d, sender, to):
        buffer, count, slot, at = (
            (k3, 256, sender % 2, 0),
            (k4, 128, sender % 4, d),
            (k5, 64, sender, 3 + d),
        )[which]
        piece = buffer.at[pl.ds(pl.multiple_of(slot * count, 64), count)]
        return remote(piece, piece, z_send.at[at], z_got.at[at], (plane + to * GROUP + me, tp))

    def z_each(act_on):
        for d in range(ZED - 1, 0, -1):
            if d == 1:
                act_on(0, d, z3)
            if d < 4:
                act_on(1, d, z4)
            act_on(2, d, z)

    def z_start():
        sizes = (2, 4, 8)

        def one(which, d, slot):
            @pl.when(slot + d < sizes[which])
            def _():
                z_copy(which, d, z, (z + d) % ZED).start()

        z_each(one)

    def z_finish_send():
        sizes = (2, 4, 8)

        def one(which, d, slot):
            @pl.when(slot + d < sizes[which])
            def _():
                z_copy(which, d, z, (z + d) % ZED).wait_send()

        z_each(one)

    def z_finish_got():
        def one(which, d, slot):
            @pl.when(slot >= d)
            def _():
                z_copy(which, d, (z + ZED - d) % ZED, z).wait_recv()

        z_each(one)

    def finish(o, top):
        return o + jnp.where(lanes(o.shape) == 1, top, 0.0)

    tri = lanes(square) <= sublanes(square)

    def causal_pair(q0, q1, kv0, kv1, v0, v1):
        s00 = jnp.where(tri, mmt(q0, kv0), MASKED)
        s10 = mmt(q1, kv0)
        s11 = jnp.where(tri, mmt(q1, kv1), MASKED)
        t0 = jnp.max(s00, axis=1, keepdims=True)
        t1 = jnp.max(jnp.maximum(s10, s11), axis=1, keepdims=True)
        p00 = jnp.exp2((s00 - t0) * EXPONENT).astype(BF16)
        p10 = jnp.exp2((s10 - t1) * EXPONENT).astype(BF16)
        p11 = jnp.exp2((s11 - t1) * EXPONENT).astype(BF16)
        return finish(mm(p00, v0), t0), finish(mm(p10, v0) + mm(p11, v1), t1)

    def near(m, carry):
        j = (y + m + (m // 2) * (5 - 2 * m)) % 4

        def wait(s):
            remote(send.at[s], got.at[s], a_send.at[s], a_got.at[s], (base + s, tp)).wait_recv()

        wait_core = jnp.where(m == 0, 1 - core, 1)

        @pl.when(m > 0)
        def _():
            wait(2 * j)

        wait(2 * j + wait_core)
        kvs, qs, v1s, parts = [], [], [], []
        for i in range(2):
            kv = got[2 * j + i, 0:ROWS]
            packed = got[2 * j + i, ROWS : ROWS + 128].astype(F32)
            q = jnp.concatenate(
                [jnp.where(low_half, packed, 0.0), jnp.where(low_half, swap(packed), 0.0)], axis=0
            ).astype(BF16)
            kvs.append(kv)
            qs.append(q)
            v1s.append(with_ones(kv))
            parts.append((mm(choose[...], kv), mm(choose[...], q)))
        for i in range(2):
            kv, q = parts[i]
            pick_kv[j, 128 * i : 128 * i + 128] = kv[0:128].astype(BF16)
            pick_v1[j, 128 * i : 128 * i + 128] = with_ones(kv[0:128])
            pick_q[j, 128 * i : 128 * i + 128] = q[0:128].astype(BF16)

        def both(which, first, last):
            return jnp.concatenate([parts[0][which][first:last], parts[1][which][first:last]], axis=0)

        at = pl.ds(pl.multiple_of((j % 2) * 128, 128), 128)
        pick_kv[4 + j // 2, at] = both(0, 128, 192).astype(BF16)
        pick_v1[4 + j // 2, at] = with_ones(both(0, 128, 192))
        pick_q[4 + j // 2, at] = both(1, 128, 192).astype(BF16)
        k3[pl.ds(pl.multiple_of(z3 * 256 + j * 64, 64), 64)] = both(0, 192, 224).astype(BF16)
        far_q[pl.ds(pl.multiple_of(j * 64, 64), 64)] = both(1, 192, 224).astype(BF16)
        k4[pl.ds(pl.multiple_of(z4 * 128 + j * 32, 32), 32)] = both(0, 224, 240).astype(BF16)
        far_q[pl.ds(pl.multiple_of(256 + j * 32, 32), 32)] = both(1, 224, 240).astype(BF16)
        k5[pl.ds(pl.multiple_of(z * 64 + j * 16, 16), 16)] = both(0, 240, 248).astype(BF16)
        far_q[pl.ds(pl.multiple_of(384 + j * 16, 16), 16)] = both(1, 240, 248).astype(BF16)

        @pl.when(m == 3)
        def _():
            z_start()

        o0, o1 = causal_pair(qs[0], qs[1], kvs[0], kvs[1], v1s[0], v1s[1])
        near_out[2 * j] = o0
        near_out[2 * j + 1] = o1
        return carry

    lax.fori_loop(0, 4, near, 0)

    for copy in w_out:
        copy.wait_recv()
    w_on = [w_piece(w_first, 2, sibling, out_far), w_piece(w_second, 3, sibling, out_far)]
    for copy in w_on:
        copy.start()

    def picked(i, carry):
        o0, o1 = causal_pair(
            pick_q[2 * i],
            pick_q[2 * i + 1],
            pick_kv[2 * i],
            pick_kv[2 * i + 1],
            pick_v1[2 * i],
            pick_v1[2 * i + 1],
        )

        @pl.when(i < 2)
        def _():
            pick_out[4 * i, 0:128] = o0[0:128]
            pick_out[4 * i + 1, 0:128] = o0[128:256]
            pick_out[4 * i + 2, 0:128] = o1[0:128]
            pick_out[4 * i + 3, 0:128] = o1[128:256]

        @pl.when(i == 2)
        def _():
            for u in range(4):
                pick_out[u, 128:192] = o0[64 * u : 64 * u + 64]
                pick_out[4 + u, 128:192] = o1[64 * u : 64 * u + 64]

        return carry

    lax.fori_loop(0, 3, picked, 0)

    z_finish_got()
    for buffer, q_first, count, slot, first in (
        (k3, 0, 256, z3, 192),
        (k4, 256, 128, z4, 224),
        (k5, 384, 64, z, 240),
    ):
        kv = buffer[...]
        q = far_q[q_first : q_first + count]
        shape = (count, 512)
        s = jnp.where(lanes(shape) <= sublanes(shape) + slot * count, mmt(q, kv), MASKED)
        t = jnp.max(s, axis=1, keepdims=True)
        p = jnp.exp2((s - t) * EXPONENT).astype(BF16)
        o = finish(mm(p, with_ones(kv)), t)
        each = count // GROUP
        for u in range(GROUP):
            pick_out[u, first : first + each] = o[each * u : each * u + each]

    tile = (ROWS, 128)
    lane = lanes(tile)
    mine = lane == branch_of(sublanes(tile))
    covered = jnp.zeros(tile, jnp.int32)
    for b in range(1, 6):
        off = offsets[b, me] & (2**b - 1)
        hit = jnp.where(sublanes(tile) % 2**b == off, 1, 0)
        covered = jnp.where(lane == b, hit, covered)

    def split(x):
        high = x.astype(BF16)
        return high, (x - high.astype(F32)).astype(BF16)

    def mix_copy(to):
        return remote(mix_send.at[to], mix_own.at[me], m_send.at[to], m_got.at[me], (base + to, tp))

    def combine(i, carry):
        s = (me + i + 1) % GROUP
        picks = pick_out[s]
        base_out = near_out[s]
        first, rest = split(picks[:, 1:2])
        first = first.astype(F32)
        second, third = split(picks[:, 1:2] - first)
        terms = jnp.concatenate(
            [
                jnp.where(mine, first, 0.0).astype(BF16),
                jnp.where(mine, second.astype(F32), 0.0).astype(BF16),
                jnp.where(mine, third.astype(F32), 0.0).astype(BF16),
            ],
            axis=1,
        )
        spread = mm(choose_t[...], terms)
        tops = spread[:, 0:128] + spread[:, 128:256] + spread[:, 256:384]
        tops = jnp.where(lane == 0, base_out[:, 1:2], jnp.where(covered == 1, tops, MASKED))
        top = jnp.max(tops, axis=1, keepdims=True)
        share = jnp.exp2((tops - top) * EXPONENT)
        high, rest = split(share)
        back = mm(choose[...], jnp.concatenate([high, rest], axis=1))
        back = back[:, 0:128] + back[:, 128:256]
        mass = jnp.sum(jnp.where(mine, back, 0.0), axis=1, keepdims=True)
        high, rest = split(jnp.where(lane == 1, 0.0, picks) * mass)
        more = mm(choose_t[...], jnp.concatenate([high, rest], axis=1))
        both = base_out * share[:, 0:1] + more[:, 0:128] + more[:, 128:256]
        mix = both / both[:, 0:1]
        packed = jnp.where(low_half, swap(mix[0:128]), mix[128:256]).astype(BF16)

        @pl.when(i < GROUP - 1)
        def _():
            mix_send[s] = packed
            mix_copy(s).start()

        @pl.when(i == GROUP - 1)
        def _():
            mix_own[me] = packed

        return carry

    lax.fori_loop(0, GROUP, combine, 0)

    def far_copy(h):
        return remote(mix_own.at[h], mix_far.at[h], f_send.at[h], f_got.at[h], partner)

    far_copy(me).start()

    def pass_on(i, carry):
        h = (me + GROUP - 1 - i) % GROUP
        remote(mix_send.at[h], mix_own.at[h], m_send.at[h], m_got.at[h], (base + h, tp)).wait_recv()
        far_copy(h).start()
        return carry

    lax.fori_loop(0, GROUP - 1, pass_on, 0)

    def widen(blocks):
        for pair in range(GROUP // 2):
            cut = slice(128 * pair, 128 * pair + 128)
            a = blocks[2 * pair].astype(F32)
            b = blocks[2 * pair + 1].astype(F32)
            mix_wide[0:128, cut] = jnp.where(low_half, a, swap(b)).astype(BF16)
            mix_wide[128:256, cut] = jnp.where(low_half, swap(a), b).astype(BF16)

    res_copy.wait_recv()
    widen(mix_own)
    for n in range(4):
        cut = slice(256 * n, 256 * n + 256)
        hidden[:, cut] = mm(mix_wide[...], out_weight[:, cut]) + res_all[
            n // 2, :, 256 * (n % 2) : 256 * (n % 2) + 256
        ].astype(F32)
    for copy in w_on:
        copy.wait_recv()

    def far_wait(h, carry):
        far_copy(h).wait_recv()
        return carry

    lax.fori_loop(0, GROUP, far_wait, 0)
    widen(mix_far)
    squares = jnp.zeros((ROWS, 1), F32)
    for n in range(4):
        cut = slice(256 * n, 256 * n + 256)
        h = hidden[:, cut] + mm(mix_wide[...], out_far[:, cut])
        hidden[:, cut] = h
        squares = squares + jnp.sum(h * h, axis=1, keepdims=True)
    inverse = lax.rsqrt(squares / 1024.0 + 1e-5)
    for n in range(4):
        cut = slice(256 * n, 256 * n + 256)
        normed[:, cut] = (hidden[:, cut] * inverse * gain[:, cut]).astype(BF16)

    loads[0].wait()
    loads[1].wait()

    def units(n, carry):
        cut = pl.ds(pl.multiple_of(n * 256, 256), 256)
        gate = mm(normed[...], gate_w[:, cut])
        up = mm(normed[...], up_w[:, cut])
        act[:, cut] = (gate / (1.0 + jnp.exp(-gate)) * up).astype(BF16)
        return carry

    lax.fori_loop(0, 4, units, 0)
    loads[2].wait()

    d_out = []
    for n in range(2):
        cut = pl.ds(pl.multiple_of((1 - tp) * COLS + n * 256, 256), 256)
        down_send[n] = mm(act[...], down_w[:, cut]).astype(BF16)
        d_out.append(remote(down_send.at[n], down_got.at[n], d_send.at[n], d_got.at[n], partner))
        d_out[-1].start()
    for n in range(2):
        cut = pl.ds(pl.multiple_of(tp * COLS + n * 256, 256), 256)
        hidden[:, cut] = hidden[:, cut] + mm(act[...], down_w[:, cut])
    for n in range(2):
        cut = pl.ds(pl.multiple_of(tp * COLS + n * 256, 256), 256)
        d_out[n].wait_recv()
        out[:, 256 * n : 256 * n + 256] = (hidden[:, cut] + down_got[n].astype(F32)).astype(BF16)

    for copy in a_out + w_out + w_on + [res_copy] + d_out:
        copy.wait_send()
    z_finish_send()

    def mix_sent(i, carry):
        mix_copy((me + i + 1) % GROUP).wait_send()
        return carry

    lax.fori_loop(0, GROUP - 1, mix_sent, 0)

    def far_sent(h, carry):
        far_copy(h).wait_send()
        return carry

    lax.fori_loop(0, GROUP, far_sent, 0)


def shards(
    residual_in,
    queries,
    keys,
    values,
    head_offset,
    out_weight,
    norm_gain,
    gate_weight,
    up_weight,
    down_weight,
):
    vmem = pl.BlockSpec(memory_space=pltpu.VMEM)
    smem = pl.BlockSpec(memory_space=pltpu.SMEM)
    hbm = pl.BlockSpec(memory_space=pl.ANY)
    dma = pltpu.SemaphoreType.DMA
    scratch = [
        pltpu.VMEM((GROUP, 384, 128), BF16),
        pltpu.VMEM((GROUP, 384, 128), BF16),
        pltpu.VMEM((6, ROWS, 128), BF16),
        pltpu.VMEM((6, ROWS, 128), BF16),
        pltpu.VMEM((6, ROWS, 128), BF16),
        pltpu.VMEM((448, 128), BF16),
        pltpu.VMEM((512, 128), BF16),
        pltpu.VMEM((512, 128), BF16),
        pltpu.VMEM((512, 128), BF16),
        pltpu.VMEM((GROUP, ROWS, 128), F32),
        pltpu.VMEM((GROUP, ROWS, 128), F32),
        pltpu.VMEM((ROWS, ROWS), BF16),
        pltpu.VMEM((ROWS, ROWS), BF16),
        pltpu.VMEM((GROUP, 128, 128), BF16),
        pltpu.VMEM((GROUP, 128, 128), BF16),
        pltpu.VMEM((GROUP, 128, 128), BF16),
        pltpu.VMEM((ROWS, COLS), BF16),
        pltpu.VMEM((2, ROWS, COLS), BF16),
        pltpu.VMEM((512, 1024), BF16),
        pltpu.VMEM((1024, 1024), BF16),
        pltpu.VMEM((1024, 1024), BF16),
        pltpu.VMEM((1024, 1024), BF16),
        pltpu.VMEM((ROWS, 1024), F32),
        pltpu.VMEM((ROWS, 1024), BF16),
        pltpu.VMEM((ROWS, 1024), BF16),
        pltpu.VMEM((2, ROWS, 256), BF16),
        pltpu.VMEM((2, ROWS, 256), BF16),
        dma((GROUP,)),
        dma((GROUP,)),
        dma((11,)),
        dma((11,)),
        dma((GROUP,)),
        dma((GROUP,)),
        dma((GROUP,)),
        dma((GROUP,)),
        dma((4,)),
        dma((4,)),
        dma,
        dma,
        dma((2,)),
        dma((2,)),
        dma((3,)),
    ]
    return pl.pallas_call(
        layer,
        out_shape=jax.ShapeDtypeStruct((ROWS, COLS), BF16),
        in_specs=[vmem, vmem, vmem, vmem, vmem, vmem, smem, hbm, hbm, hbm],
        out_specs=vmem,
        scratch_shapes=scratch,
        compiler_params=pltpu.CompilerParams(
            collective_id=0, has_side_effects=True, vmem_limit_bytes=48 * 2**20
        ),
        name="layer",
    )(
        queries,
        keys,
        values,
        residual_in,
        out_weight,
        norm_gain.reshape(1, 1024),
        head_offset,
        gate_weight,
        up_weight,
        down_weight,
    )


def solution(mesh):
    placed = (
        P("seq", "tp"),
        P("seq", "tp"),
        P("seq", "tp"),
        P("seq", "tp"),
        P(None, "tp"),
        P("tp", None),
        P(),
        P(None, "tp"),
        P(None, "tp"),
        P("tp", None),
    )
    return jax.shard_map(
        shards, mesh=mesh, in_specs=placed, out_specs=P("seq", "tp"), check_vma=False
    )
```

```python
import math

import jax
import jax.numpy as jnp
from jax import lax
from jax.experimental import pallas as pl
from jax.experimental.pallas import tpu as pltpu
from jax.sharding import PartitionSpec as P

MESH = pl.DeviceIdType.MESH
F32 = jnp.float32
BF16 = jnp.bfloat16

ROWS = 256
COLS = 512
GROUP = 8
ZED = 8
LAG = 2
MASKED = -1e30
EXPONENT = math.log2(math.e) / 8.0


def lanes(shape):
    return lax.broadcasted_iota(jnp.int32, shape, len(shape) - 1)


def sublanes(shape):
    return lax.broadcasted_iota(jnp.int32, shape, 0)


def swap(x):
    return pltpu.roll(x, 64, 1)


def mm(a, b):
    return lax.dot_general(a, b, (((1,), (0,)), ((), ())), preferred_element_type=F32)


def mmt(a, b):
    return lax.dot_general(a, b, (((1,), (1,)), ((), ())), preferred_element_type=F32)


def with_ones(kv):
    lane = lanes(kv.shape)
    return jnp.where(lane < 64, jnp.where(lane == 0, 1.0, 0.0), kv.astype(F32)).astype(BF16)


def branch_of(i):
    one = jnp.where(i < 192, 2, jnp.where(i < 224, 3, jnp.where(i < 240, 4, jnp.where(i < 248, 5, 6))))
    return jnp.where(i < 128, 1, one)


def layer(
    q_hbm,
    k_hbm,
    v_hbm,
    res_hbm,
    out_hbm,
    gain_hbm,
    offsets,
    gate_hbm,
    up_hbm,
    down_hbm,
    out,
    queries,
    keys,
    values,
    gain,
    out_weight,
    send,
    got,
    pick_kv,
    pick_v1,
    pick_q,
    far_q,
    k3,
    k4,
    k5,
    near_out,
    pick_out,
    choose,
    choose_t,
    mix_send,
    mix_own,
    mix_far,
    mix_wide,
    res_all,
    out_far,
    gate_w,
    up_w,
    down_w,
    hidden,
    normed,
    act,
    down_send,
    down_got,
    shares,
    a_send,
    a_got,
    z_send,
    z_got,
    m_send,
    m_got,
    f_send,
    f_got,
    w_send,
    w_got,
    r_send,
    r_got,
    d_send,
    d_got,
    local,
):
    seq = lax.axis_index("seq")
    tp = lax.axis_index("tp")
    base = (seq // GROUP) * GROUP
    me = seq % GROUP
    y = me // 2
    core = me % 2
    z = (seq // GROUP) % ZED
    half = seq // (GROUP * ZED)
    plane = half * (GROUP * ZED)
    partner = (seq, 1 - tp)
    behind = ((1 - half) * (GROUP * ZED) + seq % (GROUP * ZED), 1 - tp)
    sibling = (base + me + 1 - 2 * core, tp)

    def remote(src, dst, s, r, to):
        return pltpu.make_async_remote_copy(
            src_ref=src, dst_ref=dst, send_sem=s, recv_sem=r, device_id=to, device_id_type=MESH
        )

    loads = [
        pltpu.make_async_copy(src, dst, local.at[i])
        for i, (src, dst) in enumerate(
            (
                (gate_hbm, gate_w),
                (up_hbm, up_w),
                (down_hbm, down_w),
                (k_hbm, keys),
                (v_hbm, values),
                (q_hbm, queries),
                (out_hbm, out_weight),
                (res_hbm, res_all.at[tp]),
                (gain_hbm, gain),
            )
        )
    ]
    for load in loads[3:6]:
        load.start()

    k3[...] = jnp.zeros_like(k3)
    k4[...] = jnp.zeros_like(k4)
    k5[...] = jnp.zeros_like(k5)
    barrier = pltpu.get_barrier_semaphore()
    for k in range(1, GROUP):
        pl.semaphore_signal(barrier, inc=1, device_id=(base + (me + k) % GROUP, tp), device_id_type=MESH)
    for d in range(1, ZED):
        pl.semaphore_signal(
            barrier, inc=1, device_id=(plane + ((z + d) % ZED) * GROUP + me, tp), device_id_type=MESH
        )
    pl.semaphore_signal(barrier, inc=1, device_id=partner, device_id_type=MESH)
    pl.semaphore_signal(barrier, inc=1, device_id=behind, device_id_type=MESH)

    low = lanes((ROWS, 128)) < 64
    low_half = lanes((128, 128)) < 64

    def pack(pair):
        cut = pl.ds(pl.multiple_of(128 * pair, 128), 128)
        k = keys[:, cut].astype(F32)
        v = values[:, cut].astype(F32)
        q = queries[:, cut].astype(F32)
        send[2 * pair, 0:ROWS] = jnp.where(low, k, swap(v)).astype(BF16)
        send[2 * pair + 1, 0:ROWS] = jnp.where(low, swap(k), v).astype(BF16)
        top, bottom = q[0:128], q[128:256]
        send[2 * pair, ROWS : ROWS + 128] = jnp.where(low_half, top, swap(bottom)).astype(BF16)
        send[2 * pair + 1, ROWS : ROWS + 128] = jnp.where(low_half, swap(top), bottom).astype(BF16)

    def block_copy(to):
        return remote(send.at[to], got.at[me], a_send.at[to], a_got.at[me], (base + to, tp))

    for load in loads[3:6]:
        load.wait()
    pack((y + 2) % 4)
    pl.semaphore_wait(barrier, 2 * (GROUP - 1) + 2)

    def post(step):
        for c in range(2):
            block_copy(((y + step) % 4) * 2 + c).start()

    post(2)
    pack((y + 1) % 4)
    post(1)
    pack((y + 3) % 4)
    post(3)
    pack(y)
    a_last = block_copy(me + 1 - 2 * core)
    a_last.start()
    got[me] = send[me]

    w_first = core * 128
    w_second = 256 + core * 128

    def w_piece(first, i, to, src):
        piece = pl.ds(pl.multiple_of(first, 128), 128)
        return remote(src.at[piece], out_far.at[piece], w_send.at[i], w_got.at[i], to)

    w_out = [w_piece(w_first, 0, partner, out_hbm), w_piece(w_second, 1, behind, out_hbm)]
    res_copy = remote(res_hbm, res_all.at[tp], r_send, r_got, partner)
    res_copy.start()
    for copy in w_out:
        copy.start()
    for load in loads[0:3] + loads[6:]:
        load.start()

    def target(i):
        spot = jnp.full(i.shape, -1, jnp.int32)
        first = 0
        for b in range(1, 6):
            rate = 2**b
            count = ROWS // rate
            off = offsets[b, me] & (rate - 1)
            inside = (i >= first) & (i < first + count)
            spot = jnp.where(inside, (i - first) * rate + off, spot)
            first += count
        return spot

    square = (ROWS, ROWS)
    choose[...] = jnp.where(lanes(square) == target(sublanes(square)), 1.0, 0.0).astype(BF16)
    choose_t[...] = jnp.where(sublanes(square) == target(lanes(square)), 1.0, 0.0).astype(BF16)
    pick_out[:, 248:256] = jnp.zeros((GROUP, 8, 128), F32)

    z3 = z % 2
    z4 = z % 4

    def z_copy(which, d, sender, to):
        buffer, count, slot, at = (
            (k3, 256, sender % 2, 0),
            (k4, 128, sender % 4, d),
            (k5, 64, sender, 3 + d),
        )[which]
        piece = buffer.at[pl.ds(pl.multiple_of(slot * count, 64), count)]
        return remote(piece, piece, z_send.at[at], z_got.at[at], (plane + to * GROUP + me, tp))

    def z_each(act_on):
        for d in range(ZED - 1, 0, -1):
            if d == 1:
                act_on(0, d, z3)
            if d < 4:
                act_on(1, d, z4)
            act_on(2, d, z)

    def z_start():
        sizes = (2, 4, 8)

        def one(which, d, slot):
            @pl.when(slot + d < sizes[which])
            def _():
                z_copy(which, d, z, (z + d) % ZED).start()

        z_each(one)

    def z_finish_send():
        sizes = (2, 4, 8)

        def one(which, d, slot):
            @pl.when(slot + d < sizes[which])
            def _():
                z_copy(which, d, z, (z + d) % ZED).wait_send()

        z_each(one)

    def z_finish_got():
        def one(which, d, slot):
            @pl.when(slot >= d)
            def _():
                z_copy(which, d, (z + ZED - d) % ZED, z).wait_recv()

        z_each(one)

    def finish(o, top):
        return o + jnp.where(lanes(o.shape) == 1, top, 0.0)

    tri = lanes(square) <= sublanes(square)

    def causal_pair(q0, q1, kv0, kv1, v0, v1):
        s00 = jnp.where(tri, mmt(q0, kv0), MASKED)
        s10 = mmt(q1, kv0)
        s11 = jnp.where(tri, mmt(q1, kv1), MASKED)
        t0 = jnp.max(s00, axis=1, keepdims=True)
        t1 = jnp.max(jnp.maximum(s10, s11), axis=1, keepdims=True)
        p00 = jnp.exp2((s00 - t0) * EXPONENT).astype(BF16)
        p10 = jnp.exp2((s10 - t1) * EXPONENT).astype(BF16)
        p11 = jnp.exp2((s11 - t1) * EXPONENT).astype(BF16)
        return finish(mm(p00, v0), t0), finish(mm(p10, v0) + mm(p11, v1), t1)

    def near(m, carry):
        j = (y + (m % 3 + 1) * ((m + 3) // 4)) % 4

        def wait(s):
            remote(send.at[s], got.at[s], a_send.at[s], a_got.at[s], (base + s, tp)).wait_recv()

        wait_core = jnp.where(m == 0, 1 - core, 1)

        @pl.when(m > 0)
        def _():
            wait(2 * j)

        wait(2 * j + wait_core)
        kvs, qs, v1s, parts = [], [], [], []
        for i in range(2):
            kv = got[2 * j + i, 0:ROWS]
            packed = got[2 * j + i, ROWS : ROWS + 128].astype(F32)
            q = jnp.concatenate(
                [jnp.where(low_half, packed, 0.0), jnp.where(low_half, swap(packed), 0.0)], axis=0
            ).astype(BF16)
            kvs.append(kv)
            qs.append(q)
            v1s.append(with_ones(kv))
            parts.append((mm(choose[...], kv), mm(choose[...], q)))
        for i in range(2):
            kv, q = parts[i]
            pick_kv[j, 128 * i : 128 * i + 128] = kv[0:128].astype(BF16)
            pick_v1[j, 128 * i : 128 * i + 128] = with_ones(kv[0:128])
            pick_q[j, 128 * i : 128 * i + 128] = q[0:128].astype(BF16)

        def both(which, first, last):
            return jnp.concatenate([parts[0][which][first:last], parts[1][which][first:last]], axis=0)

        at = pl.ds(pl.multiple_of((j % 2) * 128, 128), 128)
        pick_kv[4 + j // 2, at] = both(0, 128, 192).astype(BF16)
        pick_v1[4 + j // 2, at] = with_ones(both(0, 128, 192))
        pick_q[4 + j // 2, at] = both(1, 128, 192).astype(BF16)
        k3[pl.ds(pl.multiple_of(z3 * 256 + j * 64, 64), 64)] = both(0, 192, 224).astype(BF16)
        far_q[pl.ds(pl.multiple_of(j * 64, 64), 64)] = both(1, 192, 224).astype(BF16)
        k4[pl.ds(pl.multiple_of(z4 * 128 + j * 32, 32), 32)] = both(0, 224, 240).astype(BF16)
        far_q[pl.ds(pl.multiple_of(256 + j * 32, 32), 32)] = both(1, 224, 240).astype(BF16)
        k5[pl.ds(pl.multiple_of(z * 64 + j * 16, 16), 16)] = both(0, 240, 248).astype(BF16)
        far_q[pl.ds(pl.multiple_of(384 + j * 16, 16), 16)] = both(1, 240, 248).astype(BF16)

        @pl.when(m == 3)
        def _():
            z_start()

        o0, o1 = causal_pair(qs[0], qs[1], kvs[0], kvs[1], v1s[0], v1s[1])
        near_out[2 * j] = o0
        near_out[2 * j + 1] = o1
        return carry

    lax.fori_loop(0, 4, near, 0)

    for copy in w_out:
        copy.wait_recv()
    w_on = [w_piece(w_first, 2, sibling, out_far), w_piece(w_second, 3, sibling, out_far)]
    for copy in w_on:
        copy.start()

    def picked(i, carry):
        o0, o1 = causal_pair(
            pick_q[2 * i],
            pick_q[2 * i + 1],
            pick_kv[2 * i],
            pick_kv[2 * i + 1],
            pick_v1[2 * i],
            pick_v1[2 * i + 1],
        )

        @pl.when(i < 2)
        def _():
            pick_out[4 * i, 0:128] = o0[0:128]
            pick_out[4 * i + 1, 0:128] = o0[128:256]
            pick_out[4 * i + 2, 0:128] = o1[0:128]
            pick_out[4 * i + 3, 0:128] = o1[128:256]

        @pl.when(i == 2)
        def _():
            for u in range(4):
                pick_out[u, 128:192] = o0[64 * u : 64 * u + 64]
                pick_out[4 + u, 128:192] = o1[64 * u : 64 * u + 64]

        return carry

    lax.fori_loop(0, 3, picked, 0)

    z_finish_got()
    for buffer, q_first, count, slot, first in (
        (k3, 0, 256, z3, 192),
        (k4, 256, 128, z4, 224),
        (k5, 384, 64, z, 240),
    ):
        kv = buffer[...]
        q = far_q[q_first : q_first + count]
        shape = (count, 512)
        s = jnp.where(lanes(shape) <= sublanes(shape) + slot * count, mmt(q, kv), MASKED)
        t = jnp.max(s, axis=1, keepdims=True)
        p = jnp.exp2((s - t) * EXPONENT).astype(BF16)
        o = finish(mm(p, with_ones(kv)), t)
        each = count // GROUP
        for u in range(GROUP):
            pick_out[u, first : first + each] = o[each * u : each * u + each]

    tile = (ROWS, 128)
    lane = lanes(tile)
    branch = branch_of(sublanes(tile))
    mine = lane % 16 == branch
    covered = jnp.zeros(tile, jnp.int32)
    for b in range(1, 6):
        off = offsets[b, me] & (2**b - 1)
        hit = jnp.where(sublanes(tile) % 2**b == off, 1, 0)
        covered = jnp.where(lane % 16 == b, hit, covered)

    def split(x):
        high = x.astype(BF16)
        return high, (x - high.astype(F32)).astype(BF16)

    tops = jnp.zeros(tile, F32)
    bases = jnp.zeros(tile, F32)
    for s in range(GROUP):
        here = lane // 16 == s
        tops = jnp.where(here, pick_out[s, :, 1:2], tops)
        bases = jnp.where(here, near_out[s, :, 1:2], bases)
    first, rest = split(jnp.where(mine, tops, 0.0))
    second, third = split(jnp.where(mine, tops, 0.0) - first.astype(F32))
    spread = mm(choose_t[...], jnp.concatenate([first, second, third], axis=1))
    tops = spread[:, 0:128] + spread[:, 128:256] + spread[:, 256:384]
    tops = jnp.where(lane % 16 == 0, bases, jnp.where(covered == 1, tops, MASKED))
    top = tops
    for shift in (1, 2, 4):
        top = jnp.maximum(top, pltpu.roll(top, shift, 1))
    for shift in (127, 126, 124):
        top = jnp.maximum(top, pltpu.roll(top, shift, 1))
    share = jnp.exp2((tops - top) * EXPONENT)
    high, rest = split(share)
    back = mm(choose[...], jnp.concatenate([high, rest], axis=1))
    shares[0] = share
    shares[1] = jnp.where(mine, back[:, 0:128] + back[:, 128:256], 0.0)

    def mix_copy(to):
        return remote(mix_send.at[to], mix_own.at[me], m_send.at[to], m_got.at[me], (base + to, tp))

    def mix_wait(h):
        remote(mix_send.at[h], mix_own.at[h], m_send.at[h], m_got.at[h], (base + h, tp)).wait_recv()

    def far_copy(h, r):
        return remote(
            mix_own.at[h, r], mix_far.at[h, r], f_send.at[2 * h + r], f_got.at[2 * h + r], partner
        )

    small = lanes((64, 128)) < 64

    def combine(i, carry):
        s = (me + i + 1) % GROUP
        here = lane // 16 == s
        near_share = jnp.sum(jnp.where(lane == 16 * s, shares[0], 0.0), axis=1, keepdims=True)
        mass = jnp.sum(jnp.where(here, shares[1], 0.0), axis=1, keepdims=True)
        both = near_out[s] * near_share + mm(choose_t[...], (pick_out[s] * mass).astype(BF16))
        mix = both / both[:, 0:1]
        halves = [
            jnp.where(small, swap(mix[128 * r : 128 * r + 64]), mix[128 * r + 64 : 128 * r + 128]).astype(
                BF16
            )
            for r in range(2)
        ]

        @pl.when(i < GROUP - 1)
        def _():
            for r in range(2):
                mix_send[s, r] = halves[r]
            mix_copy(s).start()

        @pl.when(i == GROUP - 1)
        def _():
            for r in range(2):
                mix_own[me, r] = halves[r]
            far_copy(me, 0).start()

        @pl.when(i >= LAG)
        def _():
            h = (me + GROUP - 1 - (i - LAG)) % GROUP
            mix_wait(h)
            far_copy(h, 0).start()

        return carry

    lax.fori_loop(0, GROUP, combine, 0)

    def pass_on(i, carry):
        h = (me + GROUP - 1 - i) % GROUP
        mix_wait(h)
        far_copy(h, 0).start()
        return carry

    lax.fori_loop(GROUP - LAG, GROUP - 1, pass_on, 0)

    def pass_second(h, carry):
        far_copy(h, 1).start()
        return carry

    lax.fori_loop(0, GROUP, pass_second, 0)

    def widen(blocks, r):
        for pair in range(GROUP // 2):
            cut = slice(128 * pair, 128 * pair + 128)
            a = blocks[2 * pair, r].astype(F32)
            b = blocks[2 * pair + 1, r].astype(F32)
            mix_wide[r, 0:64, cut] = jnp.where(small, a, swap(b)).astype(BF16)
            mix_wide[r, 64:128, cut] = jnp.where(small, swap(a), b).astype(BF16)

    res_copy.wait_recv()
    for load in loads[6:]:
        load.wait()

    def near_hidden(r, carry):
        widen(mix_own, r)
        for n in range(4):
            cut = slice(256 * n, 256 * n + 256)
            rows = pl.ds(pl.multiple_of(128 * r, 128), 128)
            half_cut = slice(256 * (n % 2), 256 * (n % 2) + 256)
            hidden[r, :, cut] = mm(mix_wide[r], out_weight[:, cut]) + res_all[
                n // 2, rows, half_cut
            ].astype(F32)
        return carry

    lax.fori_loop(0, 2, near_hidden, 0)
    for copy in w_on:
        copy.wait_recv()
    for load in loads[0:3]:
        load.wait()

    def down_copy(r, n):
        return remote(
            down_send.at[r, n], down_got.at[r, n], d_send.at[2 * r + n], d_got.at[2 * r + n], partner
        )

    def feed(r, carry):
        def far_wait(h, carry):
            far_copy(h, r).wait_recv()
            return carry

        lax.fori_loop(0, GROUP, far_wait, 0)
        widen(mix_far, r)
        squares = jnp.zeros((128, 1), F32)
        for n in range(4):
            cut = slice(256 * n, 256 * n + 256)
            h = hidden[r, :, cut] + mm(mix_wide[r], out_far[:, cut])
            hidden[r, :, cut] = h
            squares = squares + jnp.sum(h * h, axis=1, keepdims=True)
        inverse = lax.rsqrt(squares / 1024.0 + 1e-5)
        for n in range(4):
            cut = slice(256 * n, 256 * n + 256)
            normed[r, :, cut] = (hidden[r, :, cut] * inverse * gain[:, cut]).astype(BF16)
        for n in range(4):
            cut = slice(256 * n, 256 * n + 256)
            gate = mm(normed[r], gate_w[:, cut])
            up = mm(normed[r], up_w[:, cut])
            act[r, :, cut] = (gate / (1.0 + jnp.exp(-gate)) * up).astype(BF16)
        for n in range(2):
            cut = pl.ds(pl.multiple_of((1 - tp) * COLS + n * 256, 256), 256)
            down_send[r, n] = mm(act[r], down_w[:, cut]).astype(BF16)
            down_copy(r, n).start()
        return carry

    lax.fori_loop(0, 2, feed, 0)

    def last(r, carry):
        rows = pl.ds(pl.multiple_of(128 * r, 128), 128)
        for n in range(2):
            cut = pl.ds(pl.multiple_of(tp * COLS + n * 256, 256), 256)
            own = hidden[r, :, cut] + mm(act[r], down_w[:, cut])
            down_copy(r, n).wait_recv()
            out[rows, 256 * n : 256 * n + 256] = (own + down_got[r, n].astype(F32)).astype(BF16)
        return carry

    lax.fori_loop(0, 2, last, 0)

    def block_sent(k, carry):
        block_copy((me + k) % GROUP).wait_send()
        return carry

    lax.fori_loop(1, GROUP, block_sent, 0)
    for copy in w_out + w_on + [res_copy]:
        copy.wait_send()
    z_finish_send()

    def mix_sent(i, carry):
        mix_copy((me + i + 1) % GROUP).wait_send()
        return carry

    lax.fori_loop(0, GROUP - 1, mix_sent, 0)

    def far_sent(h, carry):
        for r in range(2):
            far_copy(h, r).wait_send()
        return carry

    lax.fori_loop(0, GROUP, far_sent, 0)
    for r in range(2):
        for n in range(2):
            down_copy(r, n).wait_send()


def shards(
    residual_in,
    queries,
    keys,
    values,
    head_offset,
    out_weight,
    norm_gain,
    gate_weight,
    up_weight,
    down_weight,
):
    vmem = pl.BlockSpec(memory_space=pltpu.VMEM)
    smem = pl.BlockSpec(memory_space=pltpu.SMEM)
    hbm = pl.BlockSpec(memory_space=pl.ANY)
    dma = pltpu.SemaphoreType.DMA
    scratch = [
        pltpu.VMEM((ROWS, COLS), BF16),
        pltpu.VMEM((ROWS, COLS), BF16),
        pltpu.VMEM((ROWS, COLS), BF16),
        pltpu.VMEM((1, 1024), F32),
        pltpu.VMEM((512, 1024), BF16),
        pltpu.VMEM((GROUP, 384, 128), BF16),
        pltpu.VMEM((GROUP, 384, 128), BF16),
        pltpu.VMEM((6, ROWS, 128), BF16),
        pltpu.VMEM((6, ROWS, 128), BF16),
        pltpu.VMEM((6, ROWS, 128), BF16),
        pltpu.VMEM((448, 128), BF16),
        pltpu.VMEM((512, 128), BF16),
        pltpu.VMEM((512, 128), BF16),
        pltpu.VMEM((512, 128), BF16),
        pltpu.VMEM((GROUP, ROWS, 128), F32),
        pltpu.VMEM((GROUP, ROWS, 128), F32),
        pltpu.VMEM((ROWS, ROWS), BF16),
        pltpu.VMEM((ROWS, ROWS), BF16),
        pltpu.VMEM((GROUP, 2, 64, 128), BF16),
        pltpu.VMEM((GROUP, 2, 64, 128), BF16),
        pltpu.VMEM((GROUP, 2, 64, 128), BF16),
        pltpu.VMEM((2, 128, COLS), BF16),
        pltpu.VMEM((2, ROWS, COLS), BF16),
        pltpu.VMEM((512, 1024), BF16),
        pltpu.VMEM((1024, 1024), BF16),
        pltpu.VMEM((1024, 1024), BF16),
        pltpu.VMEM((1024, 1024), BF16),
        pltpu.VMEM((2, 128, 1024), F32),
        pltpu.VMEM((2, 128, 1024), BF16),
        pltpu.VMEM((2, 128, 1024), BF16),
        pltpu.VMEM((2, 2, 128, 256), BF16),
        pltpu.VMEM((2, 2, 128, 256), BF16),
        pltpu.VMEM((2, ROWS, 128), F32),
        dma((GROUP,)),
        dma((GROUP,)),
        dma((11,)),
        dma((11,)),
        dma((GROUP,)),
        dma((GROUP,)),
        dma((2 * GROUP,)),
        dma((2 * GROUP,)),
        dma((4,)),
        dma((4,)),
        dma,
        dma,
        dma((4,)),
        dma((4,)),
        dma((9,)),
    ]
    return pl.pallas_call(
        layer,
        out_shape=jax.ShapeDtypeStruct((ROWS, COLS), BF16),
        in_specs=[hbm, hbm, hbm, hbm, hbm, hbm, smem, hbm, hbm, hbm],
        out_specs=vmem,
        scratch_shapes=scratch,
        compiler_params=pltpu.CompilerParams(
            collective_id=0, has_side_effects=True, vmem_limit_bytes=60 * 2**20
        ),
        name="layer",
    )(
        queries,
        keys,
        values,
        residual_in,
        out_weight,
        norm_gain.reshape(1, 1024),
        head_offset,
        gate_weight,
        up_weight,
        down_weight,
    )


def solution(mesh):
    placed = (
        P("seq", "tp"),
        P("seq", "tp"),
        P("seq", "tp"),
        P("seq", "tp"),
        P(None, "tp"),
        P("tp", None),
        P(),
        P(None, "tp"),
        P(None, "tp"),
        P("tp", None),
    )
    return jax.shard_map(
        shards, mesh=mesh, in_specs=placed, out_specs=P("seq", "tp"), check_vma=False
    )
```

```python
import math

import jax
import jax.numpy as jnp
from jax import lax
from jax.experimental import pallas as pl
from jax.experimental.pallas import tpu as pltpu
from jax.sharding import PartitionSpec as P

MESH = pl.DeviceIdType.MESH
F32 = jnp.float32
BF16 = jnp.bfloat16

ROWS = 256
COLS = 512
GROUP = 8
ZED = 8
MASKED = -1e30
EXPONENT = math.log2(math.e) / 8.0


def lanes(shape):
    return lax.broadcasted_iota(jnp.int32, shape, len(shape) - 1)


def sublanes(shape):
    return lax.broadcasted_iota(jnp.int32, shape, 0)


def swap(x):
    return pltpu.roll(x, 64, 1)


def mm(a, b):
    return lax.dot_general(a, b, (((1,), (0,)), ((), ())), preferred_element_type=F32)


def mmt(a, b):
    return lax.dot_general(a, b, (((1,), (1,)), ((), ())), preferred_element_type=F32)


def with_ones(kv):
    lane = lanes(kv.shape)
    return jnp.where(lane < 64, jnp.where(lane == 0, 1.0, 0.0), kv.astype(F32)).astype(BF16)


def branch_of(i):
    one = jnp.where(i < 192, 2, jnp.where(i < 224, 3, jnp.where(i < 240, 4, jnp.where(i < 248, 5, 6))))
    return jnp.where(i < 128, 1, one)


def layer(
    q_hbm,
    k_hbm,
    v_hbm,
    res_hbm,
    out_hbm,
    gain_hbm,
    offsets,
    gate_hbm,
    up_hbm,
    down_hbm,
    out,
    queries,
    keys,
    values,
    gain,
    out_weight,
    send,
    got,
    pick_kv,
    pick_v1,
    pick_q,
    far_q,
    k3,
    k4,
    k5,
    near_out,
    pick_out,
    choose,
    choose_t,
    mix_send,
    mix_own,
    mix_far,
    mix_wide,
    res_all,
    out_far,
    gate_w,
    up_w,
    down_w,
    hidden,
    normed,
    act,
    down_send,
    down_got,
    shares,
    weighed,
    a_send,
    a_got,
    z_send,
    z_got,
    m_send,
    m_got,
    f_send,
    f_got,
    w_send,
    w_got,
    r_send,
    r_got,
    d_send,
    d_got,
    local,
    here_sem,
    all_sem,
):
    seq = lax.axis_index("seq")
    tp = lax.axis_index("tp")
    base = (seq // GROUP) * GROUP
    me = seq % GROUP
    y = me // 2
    core = me % 2
    z = (seq // GROUP) % ZED
    half = seq // (GROUP * ZED)
    plane = half * (GROUP * ZED)
    partner = (seq, 1 - tp)
    behind = ((1 - half) * (GROUP * ZED) + seq % (GROUP * ZED), 1 - tp)
    sibling = (base + me + 1 - 2 * core, tp)

    def remote(src, dst, s, r, to):
        return pltpu.make_async_remote_copy(
            src_ref=src, dst_ref=dst, send_sem=s, recv_sem=r, device_id=to, device_id_type=MESH
        )

    loads = [
        pltpu.make_async_copy(src, dst, local.at[i])
        for i, (src, dst) in enumerate(
            (
                (gate_hbm, gate_w),
                (up_hbm, up_w),
                (down_hbm, down_w),
                (k_hbm, keys),
                (v_hbm, values),
                (q_hbm, queries),
                (out_hbm, out_weight),
                (res_hbm, res_all.at[tp]),
                (gain_hbm, gain),
            )
        )
    ]
    for load in loads[3:6]:
        load.start()

    k3[...] = jnp.zeros_like(k3)
    k4[...] = jnp.zeros_like(k4)
    k5[...] = jnp.zeros_like(k5)
    barrier = pltpu.get_barrier_semaphore()
    lead = me == 0

    def greet(device):
        pl.semaphore_signal(barrier, inc=1, device_id=device, device_id_type=MESH)

    for k in range(1, GROUP):
        to = (me + k) % GROUP

        @pl.when(to != 0)
        def _():
            greet((base + to, tp))

    greet(partner)
    greet(behind)

    def group_entered():
        @pl.when(lead)
        def _():
            pl.semaphore_wait(here_sem, GROUP - 1)

        @pl.when(me != 0)
        def _():
            pl.semaphore_wait(barrier, GROUP + 1)
            pl.semaphore_signal(here_sem, inc=1, device_id=(base, tp), device_id_type=MESH)

    def all_entered():
        @pl.when(lead)
        def _():
            for d in range(1, ZED):
                greet((plane + ((z + d) % ZED) * GROUP, tp))
            pl.semaphore_wait(barrier, ZED + 1)
            for k in range(1, GROUP):
                pl.semaphore_signal(all_sem, inc=1, device_id=(base + k, tp), device_id_type=MESH)

    def all_known():
        @pl.when(me != 0)
        def _():
            pl.semaphore_wait(all_sem, 1)

    low = lanes((ROWS, 128)) < 64
    low_half = lanes((128, 128)) < 64

    def pack(pair):
        cut = pl.ds(pl.multiple_of(128 * pair, 128), 128)
        k = keys[:, cut].astype(F32)
        v = values[:, cut].astype(F32)
        q = queries[:, cut].astype(F32)
        send[2 * pair, 0:ROWS] = jnp.where(low, k, swap(v)).astype(BF16)
        send[2 * pair + 1, 0:ROWS] = jnp.where(low, swap(k), v).astype(BF16)
        top, bottom = q[0:128], q[128:256]
        send[2 * pair, ROWS : ROWS + 128] = jnp.where(low_half, top, swap(bottom)).astype(BF16)
        send[2 * pair + 1, ROWS : ROWS + 128] = jnp.where(low_half, swap(top), bottom).astype(BF16)

    def block_copy(to):
        return remote(send.at[to], got.at[me], a_send.at[to], a_got.at[me], (base + to, tp))

    for load in loads[3:6]:
        load.wait()
    pack((y + 2) % 4)
    group_entered()

    def post(step):
        for c in range(2):
            block_copy(((y + step) % 4) * 2 + c).start()

    post(2)
    pack((y + 1) % 4)
    post(1)
    pack((y + 3) % 4)
    post(3)
    pack(y)
    a_last = block_copy(me + 1 - 2 * core)
    a_last.start()
    got[me] = send[me]
    all_entered()

    w_first = core * 128
    w_second = 256 + core * 128

    def w_piece(first, i, to, src):
        piece = pl.ds(pl.multiple_of(first, 128), 128)
        return remote(src.at[piece], out_far.at[piece], w_send.at[i], w_got.at[i], to)

    w_out = [w_piece(w_first, 0, partner, out_hbm), w_piece(w_second, 1, behind, out_hbm)]
    res_copy = remote(res_hbm, res_all.at[tp], r_send, r_got, partner)
    res_copy.start()
    for copy in w_out:
        copy.start()
    for load in loads[0:3] + loads[6:]:
        load.start()

    def target(i):
        spot = jnp.full(i.shape, -1, jnp.int32)
        first = 0
        for b in range(1, 6):
            rate = 2**b
            count = ROWS // rate
            off = offsets[b, me] & (rate - 1)
            inside = (i >= first) & (i < first + count)
            spot = jnp.where(inside, (i - first) * rate + off, spot)
            first += count
        return spot

    square = (ROWS, ROWS)
    choose[...] = jnp.where(lanes(square) == target(sublanes(square)), 1.0, 0.0).astype(BF16)
    choose_t[...] = jnp.where(sublanes(square) == target(lanes(square)), 1.0, 0.0).astype(BF16)
    pick_out[:, 248:256] = jnp.zeros((GROUP, 8, 128), F32)

    z3 = z % 2
    z4 = z % 4

    def z_copy(which, d, sender, to):
        buffer, count, slot, at = (
            (k3, 256, sender % 2, 0),
            (k4, 128, sender % 4, d),
            (k5, 64, sender, 3 + d),
        )[which]
        piece = buffer.at[pl.ds(pl.multiple_of(slot * count, 64), count)]
        return remote(piece, piece, z_send.at[at], z_got.at[at], (plane + to * GROUP + me, tp))

    def z_each(act_on):
        for d in range(ZED - 1, 0, -1):
            if d == 1:
                act_on(0, d, z3)
            if d < 4:
                act_on(1, d, z4)
            act_on(2, d, z)

    def z_start():
        sizes = (2, 4, 8)

        def one(which, d, slot):
            @pl.when(slot + d < sizes[which])
            def _():
                z_copy(which, d, z, (z + d) % ZED).start()

        z_each(one)

    def z_finish_send():
        sizes = (2, 4, 8)

        def one(which, d, slot):
            @pl.when(slot + d < sizes[which])
            def _():
                z_copy(which, d, z, (z + d) % ZED).wait_send()

        z_each(one)

    def z_finish_got():
        def one(which, d, slot):
            @pl.when(slot >= d)
            def _():
                z_copy(which, d, (z + ZED - d) % ZED, z).wait_recv()

        z_each(one)

    def finish(o, top):
        return o + jnp.where(lanes(o.shape) == 1, top, 0.0)

    tri = lanes(square) <= sublanes(square)

    def causal_pair(q0, q1, kv0, kv1, v0, v1):
        s00 = jnp.where(tri, mmt(q0, kv0), MASKED)
        s10 = mmt(q1, kv0)
        s11 = jnp.where(tri, mmt(q1, kv1), MASKED)
        t0 = jnp.max(s00, axis=1, keepdims=True)
        t1 = jnp.max(jnp.maximum(s10, s11), axis=1, keepdims=True)
        p00 = jnp.exp2((s00 - t0) * EXPONENT).astype(BF16)
        p10 = jnp.exp2((s10 - t1) * EXPONENT).astype(BF16)
        p11 = jnp.exp2((s11 - t1) * EXPONENT).astype(BF16)
        return finish(mm(p00, v0), t0), finish(mm(p10, v0) + mm(p11, v1), t1)

    def near(m, carry):
        j = (y + (m % 3 + 1) * ((m + 3) // 4)) % 4

        def wait(s):
            remote(send.at[s], got.at[s], a_send.at[s], a_got.at[s], (base + s, tp)).wait_recv()

        wait_core = jnp.where(m == 0, 1 - core, 1)

        @pl.when(m > 0)
        def _():
            wait(2 * j)

        wait(2 * j + wait_core)
        kvs, qs, v1s, parts = [], [], [], []
        for i in range(2):
            kv = got[2 * j + i, 0:ROWS]
            packed = got[2 * j + i, ROWS : ROWS + 128].astype(F32)
            q = jnp.concatenate(
                [jnp.where(low_half, packed, 0.0), jnp.where(low_half, swap(packed), 0.0)], axis=0
            ).astype(BF16)
            kvs.append(kv)
            qs.append(q)
            v1s.append(with_ones(kv))
            parts.append((mm(choose[...], kv), mm(choose[...], q)))
        for i in range(2):
            kv, q = parts[i]
            pick_kv[j, 128 * i : 128 * i + 128] = kv[0:128].astype(BF16)
            pick_v1[j, 128 * i : 128 * i + 128] = with_ones(kv[0:128])
            pick_q[j, 128 * i : 128 * i + 128] = q[0:128].astype(BF16)

        def both(which, first, last):
            return jnp.concatenate([parts[0][which][first:last], parts[1][which][first:last]], axis=0)

        at = pl.ds(pl.multiple_of((j % 2) * 128, 128), 128)
        pick_kv[4 + j // 2, at] = both(0, 128, 192).astype(BF16)
        pick_v1[4 + j // 2, at] = with_ones(both(0, 128, 192))
        pick_q[4 + j // 2, at] = both(1, 128, 192).astype(BF16)
        k3[pl.ds(pl.multiple_of(z3 * 256 + j * 64, 64), 64)] = both(0, 192, 224).astype(BF16)
        far_q[pl.ds(pl.multiple_of(j * 64, 64), 64)] = both(1, 192, 224).astype(BF16)
        k4[pl.ds(pl.multiple_of(z4 * 128 + j * 32, 32), 32)] = both(0, 224, 240).astype(BF16)
        far_q[pl.ds(pl.multiple_of(256 + j * 32, 32), 32)] = both(1, 224, 240).astype(BF16)
        k5[pl.ds(pl.multiple_of(z * 64 + j * 16, 16), 16)] = both(0, 240, 248).astype(BF16)
        far_q[pl.ds(pl.multiple_of(384 + j * 16, 16), 16)] = both(1, 240, 248).astype(BF16)

        @pl.when(m == 3)
        def _():
            all_known()
            z_start()

        o0, o1 = causal_pair(qs[0], qs[1], kvs[0], kvs[1], v1s[0], v1s[1])
        near_out[2 * j] = o0
        near_out[2 * j + 1] = o1
        return carry

    lax.fori_loop(0, 4, near, 0)

    for copy in w_out:
        copy.wait_recv()
    w_on = [w_piece(w_first, 2, sibling, out_far), w_piece(w_second, 3, sibling, out_far)]
    for copy in w_on:
        copy.start()

    def picked(i, carry):
        o0, o1 = causal_pair(
            pick_q[2 * i],
            pick_q[2 * i + 1],
            pick_kv[2 * i],
            pick_kv[2 * i + 1],
            pick_v1[2 * i],
            pick_v1[2 * i + 1],
        )

        @pl.when(i < 2)
        def _():
            pick_out[4 * i, 0:128] = o0[0:128]
            pick_out[4 * i + 1, 0:128] = o0[128:256]
            pick_out[4 * i + 2, 0:128] = o1[0:128]
            pick_out[4 * i + 3, 0:128] = o1[128:256]

        @pl.when(i == 2)
        def _():
            for u in range(4):
                pick_out[u, 128:192] = o0[64 * u : 64 * u + 64]
                pick_out[4 + u, 128:192] = o1[64 * u : 64 * u + 64]

        return carry

    lax.fori_loop(0, 3, picked, 0)

    z_finish_got()
    for buffer, q_first, count, slot, first in (
        (k3, 0, 256, z3, 192),
        (k4, 256, 128, z4, 224),
        (k5, 384, 64, z, 240),
    ):
        kv = buffer[...]
        q = far_q[q_first : q_first + count]
        shape = (count, 512)
        s = jnp.where(lanes(shape) <= sublanes(shape) + slot * count, mmt(q, kv), MASKED)
        t = jnp.max(s, axis=1, keepdims=True)
        p = jnp.exp2((s - t) * EXPONENT).astype(BF16)
        o = finish(mm(p, with_ones(kv)), t)
        each = count // GROUP
        for u in range(GROUP):
            pick_out[u, first : first + each] = o[each * u : each * u + each]

    tile = (ROWS, 128)
    lane = lanes(tile)
    branch = branch_of(sublanes(tile))
    mine = lane % 16 == branch
    covered = jnp.zeros(tile, jnp.int32)
    for b in range(1, 6):
        off = offsets[b, me] & (2**b - 1)
        hit = jnp.where(sublanes(tile) % 2**b == off, 1, 0)
        covered = jnp.where(lane % 16 == b, hit, covered)

    def split(x):
        high = x.astype(BF16)
        return high, (x - high.astype(F32)).astype(BF16)

    tops = jnp.zeros(tile, F32)
    bases = jnp.zeros(tile, F32)
    for s in range(GROUP):
        here = lane // 16 == s
        tops = jnp.where(here, pick_out[s, :, 1:2], tops)
        bases = jnp.where(here, near_out[s, :, 1:2], bases)
    first, rest = split(jnp.where(mine, tops, 0.0))
    second, third = split(jnp.where(mine, tops, 0.0) - first.astype(F32))
    spread = mm(choose_t[...], jnp.concatenate([first, second, third], axis=1))
    tops = spread[:, 0:128] + spread[:, 128:256] + spread[:, 256:384]
    tops = jnp.where(lane % 16 == 0, bases, jnp.where(covered == 1, tops, MASKED))
    top = tops
    for shift in (1, 2, 4):
        top = jnp.maximum(top, pltpu.roll(top, shift, 1))
    for shift in (127, 126, 124):
        top = jnp.maximum(top, pltpu.roll(top, shift, 1))
    share = jnp.exp2((tops - top) * EXPONENT)
    high, rest = split(share)
    back = mm(choose[...], jnp.concatenate([high, rest], axis=1))
    shares[0] = share
    shares[1] = jnp.where(mine, back[:, 0:128] + back[:, 128:256], 0.0)

    def mix_copy(to, r):
        return remote(
            mix_send.at[to, r],
            mix_own.at[me, r],
            m_send.at[2 * to + r],
            m_got.at[2 * me + r],
            (base + to, tp),
        )

    def mix_wait(h, r):
        remote(
            mix_send.at[h, r], mix_own.at[h, r], m_send.at[2 * h + r], m_got.at[2 * h + r], (base + h, tp)
        ).wait_recv()

    def far_copy(to, r):
        return remote(
            mix_send.at[to, r],
            mix_far.at[me, r],
            f_send.at[2 * to + r],
            f_got.at[2 * me + r],
            (base + to, 1 - tp),
        )

    def far_wait(h, r):
        remote(
            mix_send.at[h, r],
            mix_far.at[h, r],
            f_send.at[2 * h + r],
            f_got.at[2 * h + r],
            (base + h, 1 - tp),
        ).wait_recv()

    small = lanes((64, 128)) < 64

    def weigh(s, carry):
        mass = jnp.sum(jnp.where(lane // 16 == s, shares[1], 0.0), axis=1, keepdims=True)
        weighed[s] = (pick_out[s] * mass).astype(BF16)
        return carry

    lax.fori_loop(0, GROUP, weigh, 0)

    def combine(i, carry):
        r = i // GROUP
        s = (me + i + 3) % GROUP
        rows = pl.ds(pl.multiple_of(128 * r, 128), 128)
        near_share = jnp.sum(
            jnp.where(lanes((128, 128)) == 16 * s, shares[0, rows], 0.0), axis=1, keepdims=True
        )
        both = near_out[s, rows] * near_share + mm(choose_t[rows], weighed[s])
        mix = both / both[:, 0:1]
        mix_send[s, r] = jnp.where(small, swap(mix[0:64]), mix[64:128]).astype(BF16)
        far_copy(s, r).start()

        @pl.when(s != me)
        def _():
            mix_copy(s, r).start()

        @pl.when(s == me)
        def _():
            mix_own[me, r] = mix_send[me, r]

        return carry

    lax.fori_loop(0, 2 * GROUP, combine, 0)

    def widen(blocks, r):
        for pair in range(GROUP // 2):
            cut = slice(128 * pair, 128 * pair + 128)
            a = blocks[2 * pair, r].astype(F32)
            b = blocks[2 * pair + 1, r].astype(F32)
            mix_wide[r, 0:64, cut] = jnp.where(small, a, swap(b)).astype(BF16)
            mix_wide[r, 64:128, cut] = jnp.where(small, swap(a), b).astype(BF16)

    res_copy.wait_recv()
    for load in loads[6:]:
        load.wait()

    def near_hidden(r, carry):
        def own_wait(k, carry):
            mix_wait((me + k) % GROUP, r)
            return carry

        lax.fori_loop(1, GROUP, own_wait, 0)
        widen(mix_own, r)
        for n in range(4):
            cut = slice(256 * n, 256 * n + 256)
            rows = pl.ds(pl.multiple_of(128 * r, 128), 128)
            half_cut = slice(256 * (n % 2), 256 * (n % 2) + 256)
            hidden[r, :, cut] = mm(mix_wide[r], out_weight[:, cut]) + res_all[
                n // 2, rows, half_cut
            ].astype(F32)
        return carry

    lax.fori_loop(0, 2, near_hidden, 0)
    for copy in w_on:
        copy.wait_recv()
    for load in loads[0:3]:
        load.wait()

    def down_copy(r, n):
        return remote(
            down_send.at[r, n], down_got.at[r, n], d_send.at[2 * r + n], d_got.at[2 * r + n], partner
        )

    def feed(r, carry):
        def other_wait(h, carry):
            far_wait(h, r)
            return carry

        lax.fori_loop(0, GROUP, other_wait, 0)
        widen(mix_far, r)
        squares = jnp.zeros((128, 1), F32)
        for n in range(4):
            cut = slice(256 * n, 256 * n + 256)
            h = hidden[r, :, cut] + mm(mix_wide[r], out_far[:, cut])
            hidden[r, :, cut] = h
            squares = squares + jnp.sum(h * h, axis=1, keepdims=True)
        inverse = lax.rsqrt(squares / 1024.0 + 1e-5)
        for n in range(4):
            cut = slice(256 * n, 256 * n + 256)
            normed[r, :, cut] = (hidden[r, :, cut] * inverse * gain[:, cut]).astype(BF16)
        for n in range(4):
            cut = slice(256 * n, 256 * n + 256)
            gate = mm(normed[r], gate_w[:, cut])
            up = mm(normed[r], up_w[:, cut])
            act[r, :, cut] = (gate / (1.0 + jnp.exp(-gate)) * up).astype(BF16)
        for n in range(2):
            cut = pl.ds(pl.multiple_of((1 - tp) * COLS + n * 256, 256), 256)
            down_send[r, n] = mm(act[r], down_w[:, cut]).astype(BF16)
            down_copy(r, n).start()
        return carry

    lax.fori_loop(0, 2, feed, 0)

    def last(r, carry):
        rows = pl.ds(pl.multiple_of(128 * r, 128), 128)
        for n in range(2):
            cut = pl.ds(pl.multiple_of(tp * COLS + n * 256, 256), 256)
            own = hidden[r, :, cut] + mm(act[r], down_w[:, cut])
            down_copy(r, n).wait_recv()
            out[rows, 256 * n : 256 * n + 256] = (own + down_got[r, n].astype(F32)).astype(BF16)
        return carry

    lax.fori_loop(0, 2, last, 0)

    def block_sent(k, carry):
        block_copy((me + k) % GROUP).wait_send()
        return carry

    lax.fori_loop(1, GROUP, block_sent, 0)
    for copy in w_out + w_on + [res_copy]:
        copy.wait_send()
    z_finish_send()

    def mix_sent(i, carry):
        for r in range(2):
            mix_copy((me + i) % GROUP, r).wait_send()
        return carry

    lax.fori_loop(1, GROUP, mix_sent, 0)

    def far_sent(h, carry):
        for r in range(2):
            far_copy(h, r).wait_send()
        return carry

    lax.fori_loop(0, GROUP, far_sent, 0)
    for r in range(2):
        for n in range(2):
            down_copy(r, n).wait_send()


def shards(
    residual_in,
    queries,
    keys,
    values,
    head_offset,
    out_weight,
    norm_gain,
    gate_weight,
    up_weight,
    down_weight,
):
    vmem = pl.BlockSpec(memory_space=pltpu.VMEM)
    smem = pl.BlockSpec(memory_space=pltpu.SMEM)
    hbm = pl.BlockSpec(memory_space=pl.ANY)
    dma = pltpu.SemaphoreType.DMA
    scratch = [
        pltpu.VMEM((ROWS, COLS), BF16),
        pltpu.VMEM((ROWS, COLS), BF16),
        pltpu.VMEM((ROWS, COLS), BF16),
        pltpu.VMEM((1, 1024), F32),
        pltpu.VMEM((512, 1024), BF16),
        pltpu.VMEM((GROUP, 384, 128), BF16),
        pltpu.VMEM((GROUP, 384, 128), BF16),
        pltpu.VMEM((6, ROWS, 128), BF16),
        pltpu.VMEM((6, ROWS, 128), BF16),
        pltpu.VMEM((6, ROWS, 128), BF16),
        pltpu.VMEM((448, 128), BF16),
        pltpu.VMEM((512, 128), BF16),
        pltpu.VMEM((512, 128), BF16),
        pltpu.VMEM((512, 128), BF16),
        pltpu.VMEM((GROUP, ROWS, 128), F32),
        pltpu.VMEM((GROUP, ROWS, 128), F32),
        pltpu.VMEM((ROWS, ROWS), BF16),
        pltpu.VMEM((ROWS, ROWS), BF16),
        pltpu.VMEM((GROUP, 2, 64, 128), BF16),
        pltpu.VMEM((GROUP, 2, 64, 128), BF16),
        pltpu.VMEM((GROUP, 2, 64, 128), BF16),
        pltpu.VMEM((2, 128, COLS), BF16),
        pltpu.VMEM((2, ROWS, COLS), BF16),
        pltpu.VMEM((512, 1024), BF16),
        pltpu.VMEM((1024, 1024), BF16),
        pltpu.VMEM((1024, 1024), BF16),
        pltpu.VMEM((1024, 1024), BF16),
        pltpu.VMEM((2, 128, 1024), F32),
        pltpu.VMEM((2, 128, 1024), BF16),
        pltpu.VMEM((2, 128, 1024), BF16),
        pltpu.VMEM((2, 2, 128, 256), BF16),
        pltpu.VMEM((2, 2, 128, 256), BF16),
        pltpu.VMEM((2, ROWS, 128), F32),
        pltpu.VMEM((GROUP, ROWS, 128), BF16),
        dma((GROUP,)),
        dma((GROUP,)),
        dma((11,)),
        dma((11,)),
        dma((2 * GROUP,)),
        dma((2 * GROUP,)),
        dma((2 * GROUP,)),
        dma((2 * GROUP,)),
        dma((4,)),
        dma((4,)),
        dma,
        dma,
        dma((4,)),
        dma((4,)),
        dma((9,)),
        pltpu.SemaphoreType.REGULAR,
        pltpu.SemaphoreType.REGULAR,
    ]
    return pl.pallas_call(
        layer,
        out_shape=jax.ShapeDtypeStruct((ROWS, COLS), BF16),
        in_specs=[hbm, hbm, hbm, hbm, hbm, hbm, smem, hbm, hbm, hbm],
        out_specs=vmem,
        scratch_shapes=scratch,
        compiler_params=pltpu.CompilerParams(
            collective_id=0, has_side_effects=True, vmem_limit_bytes=60 * 2**20
        ),
        name="layer",
    )(
        queries,
        keys,
        values,
        residual_in,
        out_weight,
        norm_gain.reshape(1, 1024),
        head_offset,
        gate_weight,
        up_weight,
        down_weight,
    )


def solution(mesh):
    placed = (
        P("seq", "tp"),
        P("seq", "tp"),
        P("seq", "tp"),
        P("seq", "tp"),
        P(None, "tp"),
        P("tp", None),
        P(),
        P(None, "tp"),
        P(None, "tp"),
        P("tp", None),
    )
    return jax.shard_map(
        shards, mesh=mesh, in_specs=placed, out_specs=P("seq", "tp"), check_vma=False
    )
```

```python
import math

import jax
import jax.numpy as jnp
from jax import lax
from jax.experimental import pallas as pl
from jax.experimental.pallas import tpu as pltpu
from jax.sharding import PartitionSpec as P

MESH = pl.DeviceIdType.MESH
F32 = jnp.float32
BF16 = jnp.bfloat16

ROWS = 256
COLS = 512
GROUP = 8
ZED = 8
MASKED = -1e30
EXPONENT = math.log2(math.e) / 8.0


def lanes(shape):
    return lax.broadcasted_iota(jnp.int32, shape, len(shape) - 1)


def sublanes(shape):
    return lax.broadcasted_iota(jnp.int32, shape, 0)


def swap(x):
    return pltpu.roll(x, 64, 1)


def mm(a, b):
    return lax.dot_general(a, b, (((1,), (0,)), ((), ())), preferred_element_type=F32)


def mmt(a, b):
    return lax.dot_general(a, b, (((1,), (1,)), ((), ())), preferred_element_type=F32)


def with_ones(kv):
    lane = lanes(kv.shape)
    return jnp.where(lane < 64, jnp.where(lane == 0, 1.0, 0.0), kv.astype(F32)).astype(BF16)


def branch_of(i):
    one = jnp.where(i < 192, 2, jnp.where(i < 224, 3, jnp.where(i < 240, 4, jnp.where(i < 248, 5, 6))))
    return jnp.where(i < 128, 1, one)


def layer(
    q_hbm,
    k_hbm,
    v_hbm,
    res_hbm,
    out_hbm,
    gain_hbm,
    offsets,
    gate_hbm,
    up_hbm,
    down_hbm,
    out,
    queries,
    keys,
    values,
    gain,
    out_weight,
    send,
    got,
    pick_kv,
    pick_v1,
    pick_q,
    far_q,
    k3,
    k4,
    k5,
    near_out,
    pick_out,
    choose,
    choose_t,
    mix_send,
    mix_own,
    mix_far,
    mix_wide,
    res_all,
    out_far,
    gate_w,
    up_w,
    down_w,
    hidden,
    normed,
    act,
    down_send,
    down_got,
    shares,
    weighed,
    a_send,
    a_got,
    z_send,
    z_got,
    m_send,
    m_got,
    f_send,
    f_got,
    w_send,
    w_got,
    r_send,
    r_got,
    d_send,
    d_got,
    local,
    here_sem,
    all_sem,
    early_send,
    early,
    e_send,
    e_got,
):
    seq = lax.axis_index("seq")
    tp = lax.axis_index("tp")
    base = (seq // GROUP) * GROUP
    me = seq % GROUP
    y = me // 2
    core = me % 2
    z = (seq // GROUP) % ZED
    half = seq // (GROUP * ZED)
    plane = half * (GROUP * ZED)
    partner = (seq, 1 - tp)
    behind = ((1 - half) * (GROUP * ZED) + seq % (GROUP * ZED), 1 - tp)
    sibling = (base + me + 1 - 2 * core, tp)

    def remote(src, dst, s, r, to):
        return pltpu.make_async_remote_copy(
            src_ref=src, dst_ref=dst, send_sem=s, recv_sem=r, device_id=to, device_id_type=MESH
        )

    loads = [
        pltpu.make_async_copy(src, dst, local.at[i])
        for i, (src, dst) in enumerate(
            (
                (gate_hbm, gate_w),
                (up_hbm, up_w),
                (down_hbm, down_w),
                (k_hbm, keys),
                (v_hbm, values),
                (q_hbm, queries),
                (out_hbm, out_weight),
                (res_hbm, res_all.at[tp]),
                (gain_hbm, gain),
            )
        )
    ]
    for load in loads[3:6]:
        load.start()

    k3[...] = jnp.zeros_like(k3)
    k4[...] = jnp.zeros_like(k4)
    k5[...] = jnp.zeros_like(k5)
    barrier = pltpu.get_barrier_semaphore()
    lead = me == 0

    def greet(device):
        pl.semaphore_signal(barrier, inc=1, device_id=device, device_id_type=MESH)

    for k in range(1, GROUP):
        to = (me + k) % GROUP

        @pl.when(to != 0)
        def _():
            greet((base + to, tp))

    greet(partner)
    greet(behind)

    def group_entered():
        @pl.when(lead)
        def _():
            pl.semaphore_wait(here_sem, GROUP - 1)

        @pl.when(me != 0)
        def _():
            pl.semaphore_wait(barrier, GROUP + 1)
            pl.semaphore_signal(here_sem, inc=1, device_id=(base, tp), device_id_type=MESH)

    def all_entered():
        @pl.when(lead)
        def _():
            for d in range(1, ZED):
                greet((plane + ((z + d) % ZED) * GROUP, tp))
            pl.semaphore_wait(barrier, ZED + 1)
            for k in range(1, GROUP):
                pl.semaphore_signal(all_sem, inc=1, device_id=(base + k, tp), device_id_type=MESH)

    def all_known():
        @pl.when(me != 0)
        def _():
            pl.semaphore_wait(all_sem, 1)

    low = lanes((ROWS, 128)) < 64
    low_half = lanes((128, 128)) < 64

    def pack(pair):
        cut = pl.ds(pl.multiple_of(128 * pair, 128), 128)
        k = keys[:, cut].astype(F32)
        v = values[:, cut].astype(F32)
        q = queries[:, cut].astype(F32)
        send[2 * pair, 0:ROWS] = jnp.where(low, k, swap(v)).astype(BF16)
        send[2 * pair + 1, 0:ROWS] = jnp.where(low, swap(k), v).astype(BF16)
        top, bottom = q[0:128], q[128:256]
        send[2 * pair, ROWS : ROWS + 128] = jnp.where(low_half, top, swap(bottom)).astype(BF16)
        send[2 * pair + 1, ROWS : ROWS + 128] = jnp.where(low_half, swap(top), bottom).astype(BF16)

    def block_copy(to):
        return remote(send.at[to], got.at[me], a_send.at[to], a_got.at[me], (base + to, tp))

    def pick_early(head):
        wide = (64, ROWS)
        i = sublanes(wide)
        spot = jnp.full(wide, -1, jnp.int32)
        for b, first, count in ((3, 0, 32), (4, 32, 16), (5, 48, 8)):
            off = offsets[b, head] & (2**b - 1)
            spot = jnp.where((i >= first) & (i < first + count), (i - first) * 2**b + off, spot)
        rows = jnp.where(lanes(wide) == spot, 1.0, 0.0).astype(BF16)
        early_send[head] = mm(rows, send[head, 0:ROWS]).astype(BF16)

    def early_copy(to):
        return remote(early_send.at[to], early.at[me], e_send.at[to], e_got.at[me], (base + to, tp))

    def post(step, entered):
        pair = (y + step) % 4
        pack(pair)
        for c in range(2):
            pick_early(2 * pair + c)
        entered()
        for c in range(2):
            early_copy(2 * pair + c).start()
        for c in range(2):
            block_copy(2 * pair + c).start()

    for load in loads[3:6]:
        load.wait()
    post(2, group_entered)
    post(1, lambda: None)
    post(3, lambda: None)
    pack(y)
    for c in range(2):
        pick_early(2 * y + c)
    early_copy(me + 1 - 2 * core).start()
    a_last = block_copy(me + 1 - 2 * core)
    a_last.start()
    got[me] = send[me]
    early[me] = early_send[me]

    w_first = core * 128
    w_second = 256 + core * 128

    def w_piece(first, i, to, src):
        piece = pl.ds(pl.multiple_of(first, 128), 128)
        return remote(src.at[piece], out_far.at[piece], w_send.at[i], w_got.at[i], to)

    w_out = [w_piece(w_first, 0, partner, out_hbm), w_piece(w_second, 1, behind, out_hbm)]
    res_copy = remote(res_hbm, res_all.at[tp], r_send, r_got, partner)
    for load in loads[0:3] + loads[6:]:
        load.start()

    def target(i):
        spot = jnp.full(i.shape, -1, jnp.int32)
        first = 0
        for b in range(1, 6):
            rate = 2**b
            count = ROWS // rate
            off = offsets[b, me] & (rate - 1)
            inside = (i >= first) & (i < first + count)
            spot = jnp.where(inside, (i - first) * rate + off, spot)
            first += count
        return spot

    square = (ROWS, ROWS)
    choose[...] = jnp.where(lanes(square) == target(sublanes(square)), 1.0, 0.0).astype(BF16)
    choose_t[...] = jnp.where(sublanes(square) == target(lanes(square)), 1.0, 0.0).astype(BF16)
    pick_out[:, 248:256] = jnp.zeros((GROUP, 8, 128), F32)

    z3 = z % 2
    z4 = z % 4

    def z_copy(which, d, sender, to):
        buffer, count, slot, at = (
            (k3, 256, sender % 2, 0),
            (k4, 128, sender % 4, d),
            (k5, 64, sender, 3 + d),
        )[which]
        piece = buffer.at[pl.ds(pl.multiple_of(slot * count, 64), count)]
        return remote(piece, piece, z_send.at[at], z_got.at[at], (plane + to * GROUP + me, tp))

    def z_each(act_on):
        for d in range(ZED - 1, 0, -1):
            if d == 1:
                act_on(0, d, z3)
            if d < 4:
                act_on(1, d, z4)
            act_on(2, d, z)

    def z_start():
        sizes = (2, 4, 8)

        def one(which, d, slot):
            @pl.when(slot + d < sizes[which])
            def _():
                z_copy(which, d, z, (z + d) % ZED).start()

        z_each(one)

    def z_finish_send():
        sizes = (2, 4, 8)

        def one(which, d, slot):
            @pl.when(slot + d < sizes[which])
            def _():
                z_copy(which, d, z, (z + d) % ZED).wait_send()

        z_each(one)

    def z_finish_got():
        def one(which, d, slot):
            @pl.when(slot >= d)
            def _():
                z_copy(which, d, (z + ZED - d) % ZED, z).wait_recv()

        z_each(one)

    def finish(o, top):
        return o + jnp.where(lanes(o.shape) == 1, top, 0.0)

    all_entered()
    res_copy.start()
    for copy in w_out:
        copy.start()

    def early_wait(k, carry):
        h = (me + k) % GROUP
        remote(early_send.at[h], early.at[h], e_send.at[h], e_got.at[h], (base + h, tp)).wait_recv()
        return carry

    lax.fori_loop(1, GROUP, early_wait, 0)

    def place(j, carry):
        a = early[2 * j].astype(F32)
        b = early[2 * j + 1].astype(F32)

        def both(first, last):
            return jnp.concatenate([a[first:last], b[first:last]], axis=0).astype(BF16)

        k3[pl.ds(pl.multiple_of(z3 * 256 + j * 64, 64), 64)] = both(0, 32)
        k4[pl.ds(pl.multiple_of(z4 * 128 + j * 32, 32), 32)] = both(32, 48)
        k5[pl.ds(pl.multiple_of(z * 64 + j * 16, 16), 16)] = both(48, 56)
        return carry

    lax.fori_loop(0, GROUP // 2, place, 0)
    all_known()
    z_start()

    tri = lanes(square) <= sublanes(square)

    def causal_pair(q0, q1, kv0, kv1, v0, v1):
        s00 = jnp.where(tri, mmt(q0, kv0), MASKED)
        s10 = mmt(q1, kv0)
        s11 = jnp.where(tri, mmt(q1, kv1), MASKED)
        t0 = jnp.max(s00, axis=1, keepdims=True)
        t1 = jnp.max(jnp.maximum(s10, s11), axis=1, keepdims=True)
        p00 = jnp.exp2((s00 - t0) * EXPONENT).astype(BF16)
        p10 = jnp.exp2((s10 - t1) * EXPONENT).astype(BF16)
        p11 = jnp.exp2((s11 - t1) * EXPONENT).astype(BF16)
        return finish(mm(p00, v0), t0), finish(mm(p10, v0) + mm(p11, v1), t1)

    def near(m, carry):
        j = (y + (m % 3 + 1) * ((m + 3) // 4)) % 4

        def wait(s):
            remote(send.at[s], got.at[s], a_send.at[s], a_got.at[s], (base + s, tp)).wait_recv()

        wait_core = jnp.where(m == 0, 1 - core, 1)

        @pl.when(m > 0)
        def _():
            wait(2 * j)

        wait(2 * j + wait_core)
        kvs, qs, v1s, parts = [], [], [], []
        for i in range(2):
            kv = got[2 * j + i, 0:ROWS]
            packed = got[2 * j + i, ROWS : ROWS + 128].astype(F32)
            q = jnp.concatenate(
                [jnp.where(low_half, packed, 0.0), jnp.where(low_half, swap(packed), 0.0)], axis=0
            ).astype(BF16)
            kvs.append(kv)
            qs.append(q)
            v1s.append(with_ones(kv))
            parts.append((mm(choose[...], kv), mm(choose[...], q)))
        for i in range(2):
            kv, q = parts[i]
            pick_kv[j, 128 * i : 128 * i + 128] = kv[0:128].astype(BF16)
            pick_v1[j, 128 * i : 128 * i + 128] = with_ones(kv[0:128])
            pick_q[j, 128 * i : 128 * i + 128] = q[0:128].astype(BF16)

        def both(which, first, last):
            return jnp.concatenate([parts[0][which][first:last], parts[1][which][first:last]], axis=0)

        at = pl.ds(pl.multiple_of((j % 2) * 128, 128), 128)
        pick_kv[4 + j // 2, at] = both(0, 128, 192).astype(BF16)
        pick_v1[4 + j // 2, at] = with_ones(both(0, 128, 192))
        pick_q[4 + j // 2, at] = both(1, 128, 192).astype(BF16)
        far_q[pl.ds(pl.multiple_of(j * 64, 64), 64)] = both(1, 192, 224).astype(BF16)
        far_q[pl.ds(pl.multiple_of(256 + j * 32, 32), 32)] = both(1, 224, 240).astype(BF16)
        far_q[pl.ds(pl.multiple_of(384 + j * 16, 16), 16)] = both(1, 240, 248).astype(BF16)

        o0, o1 = causal_pair(qs[0], qs[1], kvs[0], kvs[1], v1s[0], v1s[1])
        near_out[2 * j] = o0
        near_out[2 * j + 1] = o1
        return carry

    lax.fori_loop(0, 4, near, 0)

    for copy in w_out:
        copy.wait_recv()
    w_on = [w_piece(w_first, 2, sibling, out_far), w_piece(w_second, 3, sibling, out_far)]
    for copy in w_on:
        copy.start()

    def picked(i, carry):
        o0, o1 = causal_pair(
            pick_q[2 * i],
            pick_q[2 * i + 1],
            pick_kv[2 * i],
            pick_kv[2 * i + 1],
            pick_v1[2 * i],
            pick_v1[2 * i + 1],
        )

        @pl.when(i < 2)
        def _():
            pick_out[4 * i, 0:128] = o0[0:128]
            pick_out[4 * i + 1, 0:128] = o0[128:256]
            pick_out[4 * i + 2, 0:128] = o1[0:128]
            pick_out[4 * i + 3, 0:128] = o1[128:256]

        @pl.when(i == 2)
        def _():
            for u in range(4):
                pick_out[u, 128:192] = o0[64 * u : 64 * u + 64]
                pick_out[4 + u, 128:192] = o1[64 * u : 64 * u + 64]

        return carry

    lax.fori_loop(0, 3, picked, 0)

    z_finish_got()
    for buffer, q_first, count, slot, first in (
        (k3, 0, 256, z3, 192),
        (k4, 256, 128, z4, 224),
        (k5, 384, 64, z, 240),
    ):
        kv = buffer[...]
        q = far_q[q_first : q_first + count]
        shape = (count, 512)
        s = jnp.where(lanes(shape) <= sublanes(shape) + slot * count, mmt(q, kv), MASKED)
        t = jnp.max(s, axis=1, keepdims=True)
        p = jnp.exp2((s - t) * EXPONENT).astype(BF16)
        o = finish(mm(p, with_ones(kv)), t)
        each = count // GROUP
        for u in range(GROUP):
            pick_out[u, first : first + each] = o[each * u : each * u + each]

    tile = (ROWS, 128)
    lane = lanes(tile)
    branch = branch_of(sublanes(tile))
    mine = lane % 16 == branch
    covered = jnp.zeros(tile, jnp.int32)
    for b in range(1, 6):
        off = offsets[b, me] & (2**b - 1)
        hit = jnp.where(sublanes(tile) % 2**b == off, 1, 0)
        covered = jnp.where(lane % 16 == b, hit, covered)

    def split(x):
        high = x.astype(BF16)
        return high, (x - high.astype(F32)).astype(BF16)

    tops = jnp.zeros(tile, F32)
    bases = jnp.zeros(tile, F32)
    for s in range(GROUP):
        here = lane // 16 == s
        tops = jnp.where(here, pick_out[s, :, 1:2], tops)
        bases = jnp.where(here, near_out[s, :, 1:2], bases)
    first, rest = split(jnp.where(mine, tops, 0.0))
    second, third = split(jnp.where(mine, tops, 0.0) - first.astype(F32))
    spread = mm(choose_t[...], jnp.concatenate([first, second, third], axis=1))
    tops = spread[:, 0:128] + spread[:, 128:256] + spread[:, 256:384]
    tops = jnp.where(lane % 16 == 0, bases, jnp.where(covered == 1, tops, MASKED))
    top = tops
    for shift in (1, 2, 4):
        top = jnp.maximum(top, pltpu.roll(top, shift, 1))
    for shift in (127, 126, 124):
        top = jnp.maximum(top, pltpu.roll(top, shift, 1))
    share = jnp.exp2((tops - top) * EXPONENT)
    high, rest = split(share)
    back = mm(choose[...], jnp.concatenate([high, rest], axis=1))
    shares[0] = share
    shares[1] = jnp.where(mine, back[:, 0:128] + back[:, 128:256], 0.0)

    def mix_copy(to, r):
        return remote(
            mix_send.at[to, r],
            mix_own.at[me, r],
            m_send.at[2 * to + r],
            m_got.at[2 * me + r],
            (base + to, tp),
        )

    def mix_wait(h, r):
        remote(
            mix_send.at[h, r], mix_own.at[h, r], m_send.at[2 * h + r], m_got.at[2 * h + r], (base + h, tp)
        ).wait_recv()

    def far_copy(to, r):
        return remote(
            mix_send.at[to, r],
            mix_far.at[me, r],
            f_send.at[2 * to + r],
            f_got.at[2 * me + r],
            (base + to, 1 - tp),
        )

    def far_wait(h, r):
        remote(
            mix_send.at[h, r],
            mix_far.at[h, r],
            f_send.at[2 * h + r],
            f_got.at[2 * h + r],
            (base + h, 1 - tp),
        ).wait_recv()

    small = lanes((64, 128)) < 64

    for s in range(GROUP):
        mass = jnp.sum(jnp.where(lane // 16 == s, shares[1], 0.0), axis=1, keepdims=True)
        weighed[:, 128 * s : 128 * s + 128] = (pick_out[s] * mass).astype(BF16)

    for r in range(2):
        rows = slice(128 * r, 128 * r + 128)
        for pair in range(GROUP // 2):
            more = mm(choose_t[rows], weighed[:, 256 * pair : 256 * pair + 256])
            for c in range(2):
                s = 2 * pair + c
                both = near_out[s, rows] * shares[0, rows, 16 * s : 16 * s + 1]
                both = both + more[:, 128 * c : 128 * c + 128]
                mix = both / both[:, 0:1]
                mix_send[s, r] = jnp.where(small, swap(mix[0:64]), mix[64:128]).astype(BF16)

        def issue(i, carry):
            s = (me + i + 3) % GROUP
            far_copy(s, r).start()

            @pl.when(s != me)
            def _():
                mix_copy(s, r).start()

            return carry

        lax.fori_loop(0, GROUP, issue, 0)
        mix_own[me, r] = mix_send[me, r]

    def widen(blocks, r):
        for pair in range(GROUP // 2):
            cut = slice(128 * pair, 128 * pair + 128)
            a = blocks[2 * pair, r].astype(F32)
            b = blocks[2 * pair + 1, r].astype(F32)
            mix_wide[r, 0:64, cut] = jnp.where(small, a, swap(b)).astype(BF16)
            mix_wide[r, 64:128, cut] = jnp.where(small, swap(a), b).astype(BF16)

    res_copy.wait_recv()
    for load in loads[6:]:
        load.wait()

    def near_hidden(r, carry):
        def own_wait(k, carry):
            mix_wait((me + k) % GROUP, r)
            return carry

        lax.fori_loop(1, GROUP, own_wait, 0)
        widen(mix_own, r)
        for n in range(4):
            cut = slice(256 * n, 256 * n + 256)
            rows = pl.ds(pl.multiple_of(128 * r, 128), 128)
            half_cut = slice(256 * (n % 2), 256 * (n % 2) + 256)
            hidden[r, :, cut] = mm(mix_wide[r], out_weight[:, cut]) + res_all[
                n // 2, rows, half_cut
            ].astype(F32)
        return carry

    lax.fori_loop(0, 2, near_hidden, 0)
    for copy in w_on:
        copy.wait_recv()
    for load in loads[0:3]:
        load.wait()

    def down_copy(r, n):
        return remote(
            down_send.at[r, n], down_got.at[r, n], d_send.at[2 * r + n], d_got.at[2 * r + n], partner
        )

    def feed(r, carry):
        def other_wait(h, carry):
            far_wait(h, r)
            return carry

        lax.fori_loop(0, GROUP, other_wait, 0)
        widen(mix_far, r)
        squares = jnp.zeros((128, 1), F32)
        for n in range(4):
            cut = slice(256 * n, 256 * n + 256)
            h = hidden[r, :, cut] + mm(mix_wide[r], out_far[:, cut])
            hidden[r, :, cut] = h
            squares = squares + jnp.sum(h * h, axis=1, keepdims=True)
        inverse = lax.rsqrt(squares / 1024.0 + 1e-5)
        for n in range(4):
            cut = slice(256 * n, 256 * n + 256)
            normed[r, :, cut] = (hidden[r, :, cut] * inverse * gain[:, cut]).astype(BF16)
        for n in range(4):
            cut = slice(256 * n, 256 * n + 256)
            gate = mm(normed[r], gate_w[:, cut])
            up = mm(normed[r], up_w[:, cut])
            act[r, :, cut] = (gate / (1.0 + jnp.exp(-gate)) * up).astype(BF16)
        for n in range(2):
            cut = pl.ds(pl.multiple_of((1 - tp) * COLS + n * 256, 256), 256)
            down_send[r, n] = mm(act[r], down_w[:, cut]).astype(BF16)
            down_copy(r, n).start()
        return carry

    lax.fori_loop(0, 2, feed, 0)

    def last(r, carry):
        rows = pl.ds(pl.multiple_of(128 * r, 128), 128)
        for n in range(2):
            cut = pl.ds(pl.multiple_of(tp * COLS + n * 256, 256), 256)
            own = hidden[r, :, cut] + mm(act[r], down_w[:, cut])
            down_copy(r, n).wait_recv()
            out[rows, 256 * n : 256 * n + 256] = (own + down_got[r, n].astype(F32)).astype(BF16)
        return carry

    lax.fori_loop(0, 2, last, 0)

    def block_sent(k, carry):
        block_copy((me + k) % GROUP).wait_send()
        early_copy((me + k) % GROUP).wait_send()
        return carry

    lax.fori_loop(1, GROUP, block_sent, 0)
    for copy in w_out + w_on + [res_copy]:
        copy.wait_send()
    z_finish_send()

    def mix_sent(i, carry):
        for r in range(2):
            mix_copy((me + i) % GROUP, r).wait_send()
        return carry

    lax.fori_loop(1, GROUP, mix_sent, 0)

    def far_sent(h, carry):
        for r in range(2):
            far_copy(h, r).wait_send()
        return carry

    lax.fori_loop(0, GROUP, far_sent, 0)
    for r in range(2):
        for n in range(2):
            down_copy(r, n).wait_send()


def shards(
    residual_in,
    queries,
    keys,
    values,
    head_offset,
    out_weight,
    norm_gain,
    gate_weight,
    up_weight,
    down_weight,
):
    vmem = pl.BlockSpec(memory_space=pltpu.VMEM)
    smem = pl.BlockSpec(memory_space=pltpu.SMEM)
    hbm = pl.BlockSpec(memory_space=pl.ANY)
    dma = pltpu.SemaphoreType.DMA
    scratch = [
        pltpu.VMEM((ROWS, COLS), BF16),
        pltpu.VMEM((ROWS, COLS), BF16),
        pltpu.VMEM((ROWS, COLS), BF16),
        pltpu.VMEM((1, 1024), F32),
        pltpu.VMEM((512, 1024), BF16),
        pltpu.VMEM((GROUP, 384, 128), BF16),
        pltpu.VMEM((GROUP, 384, 128), BF16),
        pltpu.VMEM((6, ROWS, 128), BF16),
        pltpu.VMEM((6, ROWS, 128), BF16),
        pltpu.VMEM((6, ROWS, 128), BF16),
        pltpu.VMEM((448, 128), BF16),
        pltpu.VMEM((512, 128), BF16),
        pltpu.VMEM((512, 128), BF16),
        pltpu.VMEM((512, 128), BF16),
        pltpu.VMEM((GROUP, ROWS, 128), F32),
        pltpu.VMEM((GROUP, ROWS, 128), F32),
        pltpu.VMEM((ROWS, ROWS), BF16),
        pltpu.VMEM((ROWS, ROWS), BF16),
        pltpu.VMEM((GROUP, 2, 64, 128), BF16),
        pltpu.VMEM((GROUP, 2, 64, 128), BF16),
        pltpu.VMEM((GROUP, 2, 64, 128), BF16),
        pltpu.VMEM((2, 128, COLS), BF16),
        pltpu.VMEM((2, ROWS, COLS), BF16),
        pltpu.VMEM((512, 1024), BF16),
        pltpu.VMEM((1024, 1024), BF16),
        pltpu.VMEM((1024, 1024), BF16),
        pltpu.VMEM((1024, 1024), BF16),
        pltpu.VMEM((2, 128, 1024), F32),
        pltpu.VMEM((2, 128, 1024), BF16),
        pltpu.VMEM((2, 128, 1024), BF16),
        pltpu.VMEM((2, 2, 128, 256), BF16),
        pltpu.VMEM((2, 2, 128, 256), BF16),
        pltpu.VMEM((2, ROWS, 128), F32),
        pltpu.VMEM((ROWS, GROUP * 128), BF16),
        dma((GROUP,)),
        dma((GROUP,)),
        dma((11,)),
        dma((11,)),
        dma((2 * GROUP,)),
        dma((2 * GROUP,)),
        dma((2 * GROUP,)),
        dma((2 * GROUP,)),
        dma((4,)),
        dma((4,)),
        dma,
        dma,
        dma((4,)),
        dma((4,)),
        dma((9,)),
        pltpu.SemaphoreType.REGULAR,
        pltpu.SemaphoreType.REGULAR,
        pltpu.VMEM((GROUP, 64, 128), BF16),
        pltpu.VMEM((GROUP, 64, 128), BF16),
        dma((GROUP,)),
        dma((GROUP,)),
    ]
    return pl.pallas_call(
        layer,
        out_shape=jax.ShapeDtypeStruct((ROWS, COLS), BF16),
        in_specs=[hbm, hbm, hbm, hbm, hbm, hbm, smem, hbm, hbm, hbm],
        out_specs=vmem,
        scratch_shapes=scratch,
        compiler_params=pltpu.CompilerParams(
            collective_id=0, has_side_effects=True, vmem_limit_bytes=60 * 2**20
        ),
        name="layer",
    )(
        queries,
        keys,
        values,
        residual_in,
        out_weight,
        norm_gain.reshape(1, 1024),
        head_offset,
        gate_weight,
        up_weight,
        down_weight,
    )


def solution(mesh):
    placed = (
        P("seq", "tp"),
        P("seq", "tp"),
        P("seq", "tp"),
        P("seq", "tp"),
        P(None, "tp"),
        P("tp", None),
        P(),
        P(None, "tp"),
        P(None, "tp"),
        P("tp", None),
    )
    return jax.shard_map(
        shards, mesh=mesh, in_specs=placed, out_specs=P("seq", "tp"), check_vma=False
    )
```

```python
import math

import jax
import jax.numpy as jnp
from jax import lax
from jax.experimental import pallas as pl
from jax.experimental.pallas import tpu as pltpu
from jax.sharding import PartitionSpec as P

MESH = pl.DeviceIdType.MESH
F32 = jnp.float32
BF16 = jnp.bfloat16

ROWS = 256
COLS = 512
GROUP = 8
ZED = 8
MASKED = -1e30
EXPONENT = math.log2(math.e) / 8.0


def lanes(shape):
    return lax.broadcasted_iota(jnp.int32, shape, len(shape) - 1)


def sublanes(shape):
    return lax.broadcasted_iota(jnp.int32, shape, 0)


def swap(x):
    return pltpu.roll(x, 64, 1)


def mm(a, b):
    return lax.dot_general(a, b, (((1,), (0,)), ((), ())), preferred_element_type=F32)


def mmt(a, b):
    return lax.dot_general(a, b, (((1,), (1,)), ((), ())), preferred_element_type=F32)


def with_ones(kv):
    lane = lanes(kv.shape)
    return jnp.where(lane < 64, jnp.where(lane == 0, 1.0, 0.0), kv.astype(F32)).astype(BF16)


def branch_of(i):
    one = jnp.where(i < 192, 2, jnp.where(i < 224, 3, jnp.where(i < 240, 4, jnp.where(i < 248, 5, 6))))
    return jnp.where(i < 128, 1, one)


def layer(
    q_hbm,
    k_hbm,
    v_hbm,
    res_hbm,
    out_hbm,
    gain_hbm,
    offsets,
    gate_hbm,
    up_hbm,
    down_hbm,
    out,
    queries,
    keys,
    values,
    gain,
    out_weight,
    send,
    got,
    pick_kv,
    pick_v1,
    pick_q,
    far_q,
    k3,
    k4,
    k5,
    near_out,
    pick_out,
    choose,
    choose_t,
    mix_send,
    mix_own,
    mix_far,
    mix_wide,
    res_all,
    out_far,
    gate_w,
    up_w,
    down_w,
    hidden,
    normed,
    act,
    down_send,
    down_got,
    shares,
    weighed,
    a_send,
    a_got,
    z_send,
    z_got,
    m_send,
    m_got,
    f_send,
    f_got,
    w_send,
    w_got,
    r_send,
    r_got,
    d_send,
    d_got,
    local,
    here_sem,
    all_sem,
    early_send,
    early,
    e_send,
    e_got,
):
    seq = lax.axis_index("seq")
    tp = lax.axis_index("tp")
    base = (seq // GROUP) * GROUP
    me = seq % GROUP
    y = me // 2
    core = me % 2
    z = (seq // GROUP) % ZED
    half = seq // (GROUP * ZED)
    plane = half * (GROUP * ZED)
    partner = (seq, 1 - tp)
    behind = ((1 - half) * (GROUP * ZED) + seq % (GROUP * ZED), 1 - tp)
    sibling = (base + me + 1 - 2 * core, tp)

    def remote(src, dst, s, r, to):
        return pltpu.make_async_remote_copy(
            src_ref=src, dst_ref=dst, send_sem=s, recv_sem=r, device_id=to, device_id_type=MESH
        )

    loads = [
        pltpu.make_async_copy(src, dst, local.at[i])
        for i, (src, dst) in enumerate(
            (
                (gate_hbm, gate_w),
                (up_hbm, up_w),
                (down_hbm, down_w),
                (k_hbm, keys),
                (v_hbm, values),
                (q_hbm, queries),
                (out_hbm, out_weight),
                (res_hbm, res_all.at[tp]),
                (gain_hbm, gain),
            )
        )
    ]
    for load in loads[3:6]:
        load.start()

    k3[...] = jnp.zeros_like(k3)
    k4[...] = jnp.zeros_like(k4)
    k5[...] = jnp.zeros_like(k5)
    barrier = pltpu.get_barrier_semaphore()
    lead = me == 0

    def greet(device):
        pl.semaphore_signal(barrier, inc=1, device_id=device, device_id_type=MESH)

    for k in range(1, GROUP):
        to = (me + k) % GROUP

        @pl.when(to != 0)
        def _():
            greet((base + to, tp))

    greet(partner)
    greet(behind)

    def group_entered():
        @pl.when(lead)
        def _():
            pl.semaphore_wait(here_sem, GROUP - 1)
            for d in range(1, ZED):
                greet((plane + ((z + d) % ZED) * GROUP, tp))

        @pl.when(me != 0)
        def _():
            pl.semaphore_wait(barrier, GROUP + 1)
            pl.semaphore_signal(here_sem, inc=1, device_id=(base, tp), device_id_type=MESH)

    def all_entered():
        @pl.when(lead)
        def _():
            pl.semaphore_wait(barrier, ZED + 1)
            for k in range(1, GROUP):
                pl.semaphore_signal(all_sem, inc=1, device_id=(base + k, tp), device_id_type=MESH)

    def all_known():
        @pl.when(me != 0)
        def _():
            pl.semaphore_wait(all_sem, 1)

    low = lanes((ROWS, 128)) < 64
    low_half = lanes((128, 128)) < 64

    def pack(pair):
        cut = pl.ds(pl.multiple_of(128 * pair, 128), 128)
        k = keys[:, cut].astype(F32)
        v = values[:, cut].astype(F32)
        q = queries[:, cut].astype(F32)
        send[2 * pair, 0:ROWS] = jnp.where(low, k, swap(v)).astype(BF16)
        send[2 * pair + 1, 0:ROWS] = jnp.where(low, swap(k), v).astype(BF16)
        top, bottom = q[0:128], q[128:256]
        send[2 * pair, ROWS : ROWS + 128] = jnp.where(low_half, top, swap(bottom)).astype(BF16)
        send[2 * pair + 1, ROWS : ROWS + 128] = jnp.where(low_half, swap(top), bottom).astype(BF16)

    def block_copy(to):
        return remote(send.at[to], got.at[me], a_send.at[to], a_got.at[me], (base + to, tp))

    def pick_early(head):
        wide = (64, ROWS)
        i = sublanes(wide)
        spot = jnp.full(wide, -1, jnp.int32)
        for b, first, count in ((3, 0, 32), (4, 32, 16), (5, 48, 8)):
            off = offsets[b, head] & (2**b - 1)
            spot = jnp.where((i >= first) & (i < first + count), (i - first) * 2**b + off, spot)
        rows = jnp.where(lanes(wide) == spot, 1.0, 0.0).astype(BF16)
        early_send[head] = mm(rows, send[head, 0:ROWS]).astype(BF16)

    def early_copy(to):
        return remote(early_send.at[to], early.at[me], e_send.at[to], e_got.at[me], (base + to, tp))

    def post(step, entered):
        pair = (y + step) % 4
        pack(pair)
        for c in range(2):
            pick_early(2 * pair + c)
        entered()
        for c in range(2):
            early_copy(2 * pair + c).start()
        for c in range(2):
            block_copy(2 * pair + c).start()

    for load in loads[3:6]:
        load.wait()
    post(2, group_entered)
    post(1, lambda: None)
    post(3, lambda: None)
    pack(y)
    for c in range(2):
        pick_early(2 * y + c)
    early_copy(me + 1 - 2 * core).start()
    a_last = block_copy(me + 1 - 2 * core)
    a_last.start()
    got[me] = send[me]
    early[me] = early_send[me]

    w_first = core * 128
    w_second = 256 + core * 128

    def w_piece(first, i, to, src):
        piece = pl.ds(pl.multiple_of(first, 128), 128)
        return remote(src.at[piece], out_far.at[piece], w_send.at[i], w_got.at[i], to)

    w_out = [w_piece(w_first, 0, partner, out_hbm), w_piece(w_second, 1, behind, out_hbm)]
    res_copy = remote(res_hbm, res_all.at[tp], r_send, r_got, partner)
    for load in loads[0:3] + loads[6:]:
        load.start()

    def target(i):
        spot = jnp.full(i.shape, -1, jnp.int32)
        first = 0
        for b in range(1, 6):
            rate = 2**b
            count = ROWS // rate
            off = offsets[b, me] & (rate - 1)
            inside = (i >= first) & (i < first + count)
            spot = jnp.where(inside, (i - first) * rate + off, spot)
            first += count
        return spot

    square = (ROWS, ROWS)
    choose[...] = jnp.where(lanes(square) == target(sublanes(square)), 1.0, 0.0).astype(BF16)
    choose_t[...] = jnp.where(sublanes(square) == target(lanes(square)), 1.0, 0.0).astype(BF16)
    pick_out[:, 248:256] = jnp.zeros((GROUP, 8, 128), F32)

    z3 = z % 2
    z4 = z % 4

    def z_copy(which, d, sender, to):
        buffer, count, slot, at = (
            (k3, 256, sender % 2, 0),
            (k4, 128, sender % 4, d),
            (k5, 64, sender, 3 + d),
        )[which]
        piece = buffer.at[pl.ds(pl.multiple_of(slot * count, 64), count)]
        return remote(piece, piece, z_send.at[at], z_got.at[at], (plane + to * GROUP + me, tp))

    def z_each(act_on):
        for d in range(ZED - 1, 0, -1):
            if d == 1:
                act_on(0, d, z3)
            if d < 4:
                act_on(1, d, z4)
            act_on(2, d, z)

    def z_start():
        sizes = (2, 4, 8)

        def one(which, d, slot):
            @pl.when(slot + d < sizes[which])
            def _():
                z_copy(which, d, z, (z + d) % ZED).start()

        z_each(one)

    def z_finish_send():
        sizes = (2, 4, 8)

        def one(which, d, slot):
            @pl.when(slot + d < sizes[which])
            def _():
                z_copy(which, d, z, (z + d) % ZED).wait_send()

        z_each(one)

    def z_finish_got():
        def one(which, d, slot):
            @pl.when(slot >= d)
            def _():
                z_copy(which, d, (z + ZED - d) % ZED, z).wait_recv()

        z_each(one)

    def finish(o, top):
        return o + jnp.where(lanes(o.shape) == 1, top, 0.0)

    all_entered()
    res_copy.start()
    for copy in w_out:
        copy.start()

    def early_wait(k, carry):
        h = (me + k) % GROUP
        remote(early_send.at[h], early.at[h], e_send.at[h], e_got.at[h], (base + h, tp)).wait_recv()
        return carry

    lax.fori_loop(1, GROUP, early_wait, 0)

    def place(j, carry):
        a = early[2 * j].astype(F32)
        b = early[2 * j + 1].astype(F32)

        def both(first, last):
            return jnp.concatenate([a[first:last], b[first:last]], axis=0).astype(BF16)

        k3[pl.ds(pl.multiple_of(z3 * 256 + j * 64, 64), 64)] = both(0, 32)
        k4[pl.ds(pl.multiple_of(z4 * 128 + j * 32, 32), 32)] = both(32, 48)
        k5[pl.ds(pl.multiple_of(z * 64 + j * 16, 16), 16)] = both(48, 56)
        return carry

    lax.fori_loop(0, GROUP // 2, place, 0)
    all_known()
    z_start()

    tri = lanes(square) <= sublanes(square)

    def causal_pair(q0, q1, kv0, kv1, v0, v1):
        s00 = jnp.where(tri, mmt(q0, kv0), MASKED)
        s10 = mmt(q1, kv0)
        s11 = jnp.where(tri, mmt(q1, kv1), MASKED)
        t0 = jnp.max(s00, axis=1, keepdims=True)
        t1 = jnp.max(jnp.maximum(s10, s11), axis=1, keepdims=True)
        p00 = jnp.exp2((s00 - t0) * EXPONENT).astype(BF16)
        p10 = jnp.exp2((s10 - t1) * EXPONENT).astype(BF16)
        p11 = jnp.exp2((s11 - t1) * EXPONENT).astype(BF16)
        return finish(mm(p00, v0), t0), finish(mm(p10, v0) + mm(p11, v1), t1)

    def near(m, carry):
        j = (y + (m % 3 + 1) * ((m + 3) // 4)) % 4

        def wait(s):
            remote(send.at[s], got.at[s], a_send.at[s], a_got.at[s], (base + s, tp)).wait_recv()

        wait_core = jnp.where(m == 0, 1 - core, 1)

        @pl.when(m > 0)
        def _():
            wait(2 * j)

        wait(2 * j + wait_core)
        kvs, qs, v1s, parts = [], [], [], []
        for i in range(2):
            kv = got[2 * j + i, 0:ROWS]
            packed = got[2 * j + i, ROWS : ROWS + 128].astype(F32)
            q = jnp.concatenate(
                [jnp.where(low_half, packed, 0.0), jnp.where(low_half, swap(packed), 0.0)], axis=0
            ).astype(BF16)
            kvs.append(kv)
            qs.append(q)
            v1s.append(with_ones(kv))
            parts.append((mm(choose[...], kv), mm(choose[...], q)))
        for i in range(2):
            kv, q = parts[i]
            pick_kv[j, 128 * i : 128 * i + 128] = kv[0:128].astype(BF16)
            pick_v1[j, 128 * i : 128 * i + 128] = with_ones(kv[0:128])
            pick_q[j, 128 * i : 128 * i + 128] = q[0:128].astype(BF16)

        def both(which, first, last):
            return jnp.concatenate([parts[0][which][first:last], parts[1][which][first:last]], axis=0)

        at = pl.ds(pl.multiple_of((j % 2) * 128, 128), 128)
        pick_kv[4 + j // 2, at] = both(0, 128, 192).astype(BF16)
        pick_v1[4 + j // 2, at] = with_ones(both(0, 128, 192))
        pick_q[4 + j // 2, at] = both(1, 128, 192).astype(BF16)
        far_q[pl.ds(pl.multiple_of(j * 64, 64), 64)] = both(1, 192, 224).astype(BF16)
        far_q[pl.ds(pl.multiple_of(256 + j * 32, 32), 32)] = both(1, 224, 240).astype(BF16)
        far_q[pl.ds(pl.multiple_of(384 + j * 16, 16), 16)] = both(1, 240, 248).astype(BF16)

        o0, o1 = causal_pair(qs[0], qs[1], kvs[0], kvs[1], v1s[0], v1s[1])
        near_out[2 * j] = o0
        near_out[2 * j + 1] = o1
        return carry

    lax.fori_loop(0, 4, near, 0)

    for copy in w_out:
        copy.wait_recv()
    w_on = [w_piece(w_first, 2, sibling, out_far), w_piece(w_second, 3, sibling, out_far)]
    for copy in w_on:
        copy.start()

    def picked(i, carry):
        o0, o1 = causal_pair(
            pick_q[2 * i],
            pick_q[2 * i + 1],
            pick_kv[2 * i],
            pick_kv[2 * i + 1],
            pick_v1[2 * i],
            pick_v1[2 * i + 1],
        )

        @pl.when(i < 2)
        def _():
            pick_out[4 * i, 0:128] = o0[0:128]
            pick_out[4 * i + 1, 0:128] = o0[128:256]
            pick_out[4 * i + 2, 0:128] = o1[0:128]
            pick_out[4 * i + 3, 0:128] = o1[128:256]

        @pl.when(i == 2)
        def _():
            for u in range(4):
                pick_out[u, 128:192] = o0[64 * u : 64 * u + 64]
                pick_out[4 + u, 128:192] = o1[64 * u : 64 * u + 64]

        return carry

    lax.fori_loop(0, 3, picked, 0)

    z_finish_got()
    for buffer, q_first, count, slot, first in (
        (k3, 0, 256, z3, 192),
        (k4, 256, 128, z4, 224),
        (k5, 384, 64, z, 240),
    ):
        kv = buffer[...]
        q = far_q[q_first : q_first + count]
        shape = (count, 512)
        s = jnp.where(lanes(shape) <= sublanes(shape) + slot * count, mmt(q, kv), MASKED)
        t = jnp.max(s, axis=1, keepdims=True)
        p = jnp.exp2((s - t) * EXPONENT).astype(BF16)
        o = finish(mm(p, with_ones(kv)), t)
        each = count // GROUP
        for u in range(GROUP):
            pick_out[u, first : first + each] = o[each * u : each * u + each]

    tile = (ROWS, 128)
    lane = lanes(tile)
    branch = branch_of(sublanes(tile))
    mine = lane % 16 == branch
    covered = jnp.zeros(tile, jnp.int32)
    for b in range(1, 6):
        off = offsets[b, me] & (2**b - 1)
        hit = jnp.where(sublanes(tile) % 2**b == off, 1, 0)
        covered = jnp.where(lane % 16 == b, hit, covered)

    def split(x):
        high = x.astype(BF16)
        return high, (x - high.astype(F32)).astype(BF16)

    tops = jnp.zeros(tile, F32)
    bases = jnp.zeros(tile, F32)
    for s in range(GROUP):
        here = lane // 16 == s
        tops = jnp.where(here, pick_out[s, :, 1:2], tops)
        bases = jnp.where(here, near_out[s, :, 1:2], bases)
    first, rest = split(jnp.where(mine, tops, 0.0))
    second, third = split(jnp.where(mine, tops, 0.0) - first.astype(F32))
    spread = mm(choose_t[...], jnp.concatenate([first, second, third], axis=1))
    tops = spread[:, 0:128] + spread[:, 128:256] + spread[:, 256:384]
    tops = jnp.where(lane % 16 == 0, bases, jnp.where(covered == 1, tops, MASKED))
    top = tops
    for shift in (1, 2, 4):
        top = jnp.maximum(top, pltpu.roll(top, shift, 1))
    for shift in (127, 126, 124):
        top = jnp.maximum(top, pltpu.roll(top, shift, 1))
    share = jnp.exp2((tops - top) * EXPONENT)
    high, rest = split(share)
    back = mm(choose[...], jnp.concatenate([high, rest], axis=1))
    shares[0] = share
    shares[1] = jnp.where(mine, back[:, 0:128] + back[:, 128:256], 0.0)

    def mix_copy(to, r):
        return remote(
            mix_send.at[to, r],
            mix_own.at[me, r],
            m_send.at[2 * to + r],
            m_got.at[2 * me + r],
            (base + to, tp),
        )

    def mix_wait(h, r):
        remote(
            mix_send.at[h, r], mix_own.at[h, r], m_send.at[2 * h + r], m_got.at[2 * h + r], (base + h, tp)
        ).wait_recv()

    def far_copy(to, r):
        return remote(
            mix_send.at[to, r],
            mix_far.at[me, r],
            f_send.at[2 * to + r],
            f_got.at[2 * me + r],
            (base + to, 1 - tp),
        )

    def far_wait(h, r):
        remote(
            mix_send.at[h, r],
            mix_far.at[h, r],
            f_send.at[2 * h + r],
            f_got.at[2 * h + r],
            (base + h, 1 - tp),
        ).wait_recv()

    small = lanes((64, 128)) < 64

    for s in range(GROUP):
        mass = jnp.sum(jnp.where(lane // 16 == s, shares[1], 0.0), axis=1, keepdims=True)
        weighed[:, 128 * s : 128 * s + 128] = (pick_out[s] * mass).astype(BF16)

    for r in range(2):
        rows = slice(128 * r, 128 * r + 128)
        for pair in range(GROUP // 2):
            more = mm(choose_t[rows], weighed[:, 256 * pair : 256 * pair + 256])
            for c in range(2):
                s = 2 * pair + c
                both = near_out[s, rows] * shares[0, rows, 16 * s : 16 * s + 1]
                both = both + more[:, 128 * c : 128 * c + 128]
                mix = both / both[:, 0:1]
                mix_send[s, r] = jnp.where(small, swap(mix[0:64]), mix[64:128]).astype(BF16)

        def issue(i, carry):
            s = (me + i + 3) % GROUP
            far_copy(s, r).start()
            return carry

        def issue_own(i, carry):
            mix_copy((me + i) % GROUP, r).start()
            return carry

        lax.fori_loop(0, GROUP, issue, 0)
        lax.fori_loop(1, GROUP, issue_own, 0)
        mix_own[me, r] = mix_send[me, r]

    def widen(blocks, r):
        for pair in range(GROUP // 2):
            cut = slice(128 * pair, 128 * pair + 128)
            a = blocks[2 * pair, r].astype(F32)
            b = blocks[2 * pair + 1, r].astype(F32)
            mix_wide[r, 0:64, cut] = jnp.where(small, a, swap(b)).astype(BF16)
            mix_wide[r, 64:128, cut] = jnp.where(small, swap(a), b).astype(BF16)

    res_copy.wait_recv()
    for load in loads[6:]:
        load.wait()

    def near_hidden(r, carry):
        def own_wait(k, carry):
            mix_wait((me + k) % GROUP, r)
            return carry

        lax.fori_loop(1, GROUP, own_wait, 0)
        widen(mix_own, r)
        for n in range(4):
            cut = slice(256 * n, 256 * n + 256)
            rows = pl.ds(pl.multiple_of(128 * r, 128), 128)
            half_cut = slice(256 * (n % 2), 256 * (n % 2) + 256)
            hidden[r, :, cut] = mm(mix_wide[r], out_weight[:, cut]) + res_all[
                n // 2, rows, half_cut
            ].astype(F32)
        return carry

    lax.fori_loop(0, 2, near_hidden, 0)
    for copy in w_on:
        copy.wait_recv()
    for load in loads[0:3]:
        load.wait()

    def down_copy(r, n):
        return remote(
            down_send.at[r, n], down_got.at[r, n], d_send.at[2 * r + n], d_got.at[2 * r + n], partner
        )

    def feed(r, carry):
        def other_wait(h, carry):
            far_wait(h, r)
            return carry

        lax.fori_loop(0, GROUP, other_wait, 0)
        widen(mix_far, r)
        squares = jnp.zeros((128, 1), F32)
        for n in range(4):
            cut = slice(256 * n, 256 * n + 256)
            h = hidden[r, :, cut] + mm(mix_wide[r], out_far[:, cut])
            hidden[r, :, cut] = h
            squares = squares + jnp.sum(h * h, axis=1, keepdims=True)
        inverse = lax.rsqrt(squares / 1024.0 + 1e-5)
        for n in range(4):
            cut = slice(256 * n, 256 * n + 256)
            normed[r, :, cut] = (hidden[r, :, cut] * inverse * gain[:, cut]).astype(BF16)
        for n in range(4):
            cut = slice(256 * n, 256 * n + 256)
            gate = mm(normed[r], gate_w[:, cut])
            up = mm(normed[r], up_w[:, cut])
            act[r, :, cut] = (gate / (1.0 + jnp.exp(-gate)) * up).astype(BF16)
        for n in range(2):
            cut = pl.ds(pl.multiple_of((1 - tp) * COLS + n * 256, 256), 256)
            down_send[r, n] = mm(act[r], down_w[:, cut]).astype(BF16)
            down_copy(r, n).start()
        return carry

    lax.fori_loop(0, 2, feed, 0)

    def last(r, carry):
        rows = pl.ds(pl.multiple_of(128 * r, 128), 128)
        for n in range(2):
            cut = pl.ds(pl.multiple_of(tp * COLS + n * 256, 256), 256)
            own = hidden[r, :, cut] + mm(act[r], down_w[:, cut])
            down_copy(r, n).wait_recv()
            out[rows, 256 * n : 256 * n + 256] = (own + down_got[r, n].astype(F32)).astype(BF16)
        return carry

    lax.fori_loop(0, 2, last, 0)

    def block_sent(k, carry):
        block_copy((me + k) % GROUP).wait_send()
        early_copy((me + k) % GROUP).wait_send()
        return carry

    lax.fori_loop(1, GROUP, block_sent, 0)
    for copy in w_out + w_on + [res_copy]:
        copy.wait_send()
    z_finish_send()

    def mix_sent(i, carry):
        for r in range(2):
            mix_copy((me + i) % GROUP, r).wait_send()
        return carry

    lax.fori_loop(1, GROUP, mix_sent, 0)

    def far_sent(h, carry):
        for r in range(2):
            far_copy(h, r).wait_send()
        return carry

    lax.fori_loop(0, GROUP, far_sent, 0)
    for r in range(2):
        for n in range(2):
            down_copy(r, n).wait_send()


def shards(
    residual_in,
    queries,
    keys,
    values,
    head_offset,
    out_weight,
    norm_gain,
    gate_weight,
    up_weight,
    down_weight,
):
    vmem = pl.BlockSpec(memory_space=pltpu.VMEM)
    smem = pl.BlockSpec(memory_space=pltpu.SMEM)
    hbm = pl.BlockSpec(memory_space=pl.ANY)
    dma = pltpu.SemaphoreType.DMA
    scratch = [
        pltpu.VMEM((ROWS, COLS), BF16),
        pltpu.VMEM((ROWS, COLS), BF16),
        pltpu.VMEM((ROWS, COLS), BF16),
        pltpu.VMEM((1, 1024), F32),
        pltpu.VMEM((512, 1024), BF16),
        pltpu.VMEM((GROUP, 384, 128), BF16),
        pltpu.VMEM((GROUP, 384, 128), BF16),
        pltpu.VMEM((6, ROWS, 128), BF16),
        pltpu.VMEM((6, ROWS, 128), BF16),
        pltpu.VMEM((6, ROWS, 128), BF16),
        pltpu.VMEM((448, 128), BF16),
        pltpu.VMEM((512, 128), BF16),
        pltpu.VMEM((512, 128), BF16),
        pltpu.VMEM((512, 128), BF16),
        pltpu.VMEM((GROUP, ROWS, 128), F32),
        pltpu.VMEM((GROUP, ROWS, 128), F32),
        pltpu.VMEM((ROWS, ROWS), BF16),
        pltpu.VMEM((ROWS, ROWS), BF16),
        pltpu.VMEM((GROUP, 2, 64, 128), BF16),
        pltpu.VMEM((GROUP, 2, 64, 128), BF16),
        pltpu.VMEM((GROUP, 2, 64, 128), BF16),
        pltpu.VMEM((2, 128, COLS), BF16),
        pltpu.VMEM((2, ROWS, COLS), BF16),
        pltpu.VMEM((512, 1024), BF16),
        pltpu.VMEM((1024, 1024), BF16),
        pltpu.VMEM((1024, 1024), BF16),
        pltpu.VMEM((1024, 1024), BF16),
        pltpu.VMEM((2, 128, 1024), F32),
        pltpu.VMEM((2, 128, 1024), BF16),
        pltpu.VMEM((2, 128, 1024), BF16),
        pltpu.VMEM((2, 2, 128, 256), BF16),
        pltpu.VMEM((2, 2, 128, 256), BF16),
        pltpu.VMEM((2, ROWS, 128), F32),
        pltpu.VMEM((ROWS, GROUP * 128), BF16),
        dma((GROUP,)),
        dma((GROUP,)),
        dma((11,)),
        dma((11,)),
        dma((2 * GROUP,)),
        dma((2 * GROUP,)),
        dma((2 * GROUP,)),
        dma((2 * GROUP,)),
        dma((4,)),
        dma((4,)),
        dma,
        dma,
        dma((4,)),
        dma((4,)),
        dma((9,)),
        pltpu.SemaphoreType.REGULAR,
        pltpu.SemaphoreType.REGULAR,
        pltpu.VMEM((GROUP, 64, 128), BF16),
        pltpu.VMEM((GROUP, 64, 128), BF16),
        dma((GROUP,)),
        dma((GROUP,)),
    ]
    return pl.pallas_call(
        layer,
        out_shape=jax.ShapeDtypeStruct((ROWS, COLS), BF16),
        in_specs=[hbm, hbm, hbm, hbm, hbm, hbm, smem, hbm, hbm, hbm],
        out_specs=vmem,
        scratch_shapes=scratch,
        compiler_params=pltpu.CompilerParams(
            collective_id=0, has_side_effects=True, vmem_limit_bytes=60 * 2**20
        ),
        name="layer",
    )(
        queries,
        keys,
        values,
        residual_in,
        out_weight,
        norm_gain.reshape(1, 1024),
        head_offset,
        gate_weight,
        up_weight,
        down_weight,
    )


def solution(mesh):
    placed = (
        P("seq", "tp"),
        P("seq", "tp"),
        P("seq", "tp"),
        P("seq", "tp"),
        P(None, "tp"),
        P("tp", None),
        P(),
        P(None, "tp"),
        P(None, "tp"),
        P("tp", None),
    )
    return jax.shard_map(
        shards, mesh=mesh, in_specs=placed, out_specs=P("seq", "tp"), check_vma=False
    )
```

```python
import math

import jax
import jax.numpy as jnp
from jax import lax
from jax.experimental import pallas as pl
from jax.experimental.pallas import tpu as pltpu
from jax.sharding import PartitionSpec as P

MESH = pl.DeviceIdType.MESH
F32 = jnp.float32
BF16 = jnp.bfloat16

ROWS = 256
COLS = 512
GROUP = 8
ZED = 8
MASKED = -1e30
EXPONENT = math.log2(math.e) / 8.0


def lanes(shape):
    return lax.broadcasted_iota(jnp.int32, shape, len(shape) - 1)


def sublanes(shape):
    return lax.broadcasted_iota(jnp.int32, shape, 0)


def swap(x):
    return pltpu.roll(x, 64, 1)


def mm(a, b):
    return lax.dot_general(a, b, (((1,), (0,)), ((), ())), preferred_element_type=F32)


def mmt(a, b):
    return lax.dot_general(a, b, (((1,), (1,)), ((), ())), preferred_element_type=F32)


def with_ones(kv):
    lane = lanes(kv.shape)
    return jnp.where(lane < 64, jnp.where(lane == 0, 1.0, 0.0), kv.astype(F32)).astype(BF16)


def branch_of(i):
    one = jnp.where(i < 192, 2, jnp.where(i < 224, 3, jnp.where(i < 240, 4, jnp.where(i < 248, 5, 6))))
    return jnp.where(i < 128, 1, one)


def layer(
    q_hbm,
    k_hbm,
    v_hbm,
    res_hbm,
    out_hbm,
    gain_hbm,
    offsets,
    gate_hbm,
    up_hbm,
    down_hbm,
    out,
    queries,
    keys,
    values,
    gain,
    out_weight,
    send,
    got,
    pick_kv,
    pick_v1,
    pick_q,
    far_q,
    k3,
    k4,
    k5,
    near_out,
    pick_out,
    choose,
    choose_t,
    mix_send,
    mix_own,
    mix_far,
    mix_wide,
    res_all,
    out_far,
    gate_w,
    up_w,
    down_w,
    hidden,
    normed,
    act,
    down_send,
    down_got,
    shares,
    weighed,
    a_send,
    a_got,
    z_send,
    z_got,
    m_send,
    m_got,
    f_send,
    f_got,
    w_send,
    w_got,
    r_send,
    r_got,
    d_send,
    d_got,
    local,
    here_sem,
    all_sem,
    early_send,
    early,
    e_send,
    e_got,
):
    seq = lax.axis_index("seq")
    tp = lax.axis_index("tp")
    base = (seq // GROUP) * GROUP
    me = seq % GROUP
    y = me // 2
    core = me % 2
    z = (seq // GROUP) % ZED
    half = seq // (GROUP * ZED)
    plane = half * (GROUP * ZED)
    partner = (seq, 1 - tp)
    behind = ((1 - half) * (GROUP * ZED) + seq % (GROUP * ZED), 1 - tp)
    sibling = (base + me + 1 - 2 * core, tp)

    def remote(src, dst, s, r, to):
        return pltpu.make_async_remote_copy(
            src_ref=src, dst_ref=dst, send_sem=s, recv_sem=r, device_id=to, device_id_type=MESH
        )

    loads = [
        pltpu.make_async_copy(src, dst, local.at[i])
        for i, (src, dst) in enumerate(
            (
                (gate_hbm, gate_w),
                (up_hbm, up_w),
                (down_hbm, down_w),
                (k_hbm, keys),
                (v_hbm, values),
                (q_hbm, queries),
                (out_hbm, out_weight),
                (res_hbm, res_all.at[tp]),
                (gain_hbm, gain),
            )
        )
    ]
    for load in loads[3:6]:
        load.start()

    k3[...] = jnp.zeros_like(k3)
    k4[...] = jnp.zeros_like(k4)
    k5[...] = jnp.zeros_like(k5)
    barrier = pltpu.get_barrier_semaphore()
    lead = me == 0

    def greet(device):
        pl.semaphore_signal(barrier, inc=1, device_id=device, device_id_type=MESH)

    for k in range(1, GROUP):
        to = (me + k) % GROUP

        @pl.when(to != 0)
        def _():
            greet((base + to, tp))

    greet(partner)
    greet(behind)

    def group_entered():
        @pl.when(lead)
        def _():
            pl.semaphore_wait(here_sem, GROUP - 1)
            for d in range(1, ZED):
                greet((plane + ((z + d) % ZED) * GROUP, tp))

        @pl.when(me != 0)
        def _():
            pl.semaphore_wait(barrier, GROUP + 1)
            pl.semaphore_signal(here_sem, inc=1, device_id=(base, tp), device_id_type=MESH)

    def all_entered():
        @pl.when(lead)
        def _():
            pl.semaphore_wait(barrier, ZED + 1)
            for k in range(1, GROUP):
                pl.semaphore_signal(all_sem, inc=1, device_id=(base + k, tp), device_id_type=MESH)

    def all_known():
        @pl.when(me != 0)
        def _():
            pl.semaphore_wait(all_sem, 1)

    low = lanes((ROWS, 128)) < 64
    low_half = lanes((128, 128)) < 64

    def pack(pair):
        cut = pl.ds(pl.multiple_of(128 * pair, 128), 128)
        k = keys[:, cut].astype(F32)
        v = values[:, cut].astype(F32)
        q = queries[:, cut].astype(F32)
        send[2 * pair, 0:ROWS] = jnp.where(low, k, swap(v)).astype(BF16)
        send[2 * pair + 1, 0:ROWS] = jnp.where(low, swap(k), v).astype(BF16)
        top, bottom = q[0:128], q[128:256]
        send[2 * pair, ROWS : ROWS + 128] = jnp.where(low_half, top, swap(bottom)).astype(BF16)
        send[2 * pair + 1, ROWS : ROWS + 128] = jnp.where(low_half, swap(top), bottom).astype(BF16)

    def block_copy(to):
        return remote(send.at[to], got.at[me], a_send.at[to], a_got.at[me], (base + to, tp))

    def pick_early(head):
        wide = (64, ROWS)
        i = sublanes(wide)
        spot = jnp.full(wide, -1, jnp.int32)
        for b, first, count in ((3, 0, 32), (4, 32, 16), (5, 48, 8)):
            off = offsets[b, head] & (2**b - 1)
            spot = jnp.where((i >= first) & (i < first + count), (i - first) * 2**b + off, spot)
        rows = jnp.where(lanes(wide) == spot, 1.0, 0.0).astype(BF16)
        early_send[head] = mm(rows, send[head, 0:ROWS]).astype(BF16)

    def early_copy(to):
        return remote(early_send.at[to], early.at[me], e_send.at[to], e_got.at[me], (base + to, tp))

    def post(step, entered):
        pair = (y + step) % 4
        pack(pair)
        for c in range(2):
            pick_early(2 * pair + c)
        entered()
        for c in range(2):
            early_copy(2 * pair + c).start()
        for c in range(2):
            block_copy(2 * pair + c).start()

    for load in loads[3:6]:
        load.wait()
    post(2, group_entered)
    post(1, lambda: None)
    post(3, lambda: None)
    pack(y)
    for c in range(2):
        pick_early(2 * y + c)
    early_copy(me + 1 - 2 * core).start()
    a_last = block_copy(me + 1 - 2 * core)
    a_last.start()
    got[me] = send[me]
    early[me] = early_send[me]

    w_first = core * 128
    w_second = 256 + core * 128

    def w_piece(first, i, to, src):
        piece = pl.ds(pl.multiple_of(first, 128), 128)
        return remote(src.at[piece], out_far.at[piece], w_send.at[i], w_got.at[i], to)

    w_out = [w_piece(w_first, 0, partner, out_hbm), w_piece(w_second, 1, behind, out_hbm)]
    res_copy = remote(res_hbm, res_all.at[tp], r_send, r_got, partner)
    for load in loads[0:3] + loads[6:]:
        load.start()

    def target(i):
        spot = jnp.full(i.shape, -1, jnp.int32)
        first = 0
        for b in range(1, 6):
            rate = 2**b
            count = ROWS // rate
            off = offsets[b, me] & (rate - 1)
            inside = (i >= first) & (i < first + count)
            spot = jnp.where(inside, (i - first) * rate + off, spot)
            first += count
        return spot

    square = (ROWS, ROWS)
    choose[...] = jnp.where(lanes(square) == target(sublanes(square)), 1.0, 0.0).astype(BF16)
    choose_t[...] = jnp.where(sublanes(square) == target(lanes(square)), 1.0, 0.0).astype(BF16)
    pick_out[:, 248:256] = jnp.zeros((GROUP, 8, 128), F32)

    z3 = z % 2
    z4 = z % 4

    def z_copy(which, d, sender, to):
        buffer, count, slot, at = (
            (k3, 256, sender % 2, 0),
            (k4, 128, sender % 4, d),
            (k5, 64, sender, 3 + d),
        )[which]
        piece = buffer.at[pl.ds(pl.multiple_of(slot * count, 64), count)]
        return remote(piece, piece, z_send.at[at], z_got.at[at], (plane + to * GROUP + me, tp))

    def z_each(act_on):
        for d in range(ZED - 1, 0, -1):
            if d == 1:
                act_on(0, d, z3)
            if d < 4:
                act_on(1, d, z4)
            act_on(2, d, z)

    def z_start():
        sizes = (2, 4, 8)

        def one(which, d, slot):
            @pl.when(slot + d < sizes[which])
            def _():
                z_copy(which, d, z, (z + d) % ZED).start()

        z_each(one)

    def z_finish_send():
        sizes = (2, 4, 8)

        def one(which, d, slot):
            @pl.when(slot + d < sizes[which])
            def _():
                z_copy(which, d, z, (z + d) % ZED).wait_send()

        z_each(one)

    def z_finish_got():
        def one(which, d, slot):
            @pl.when(slot >= d)
            def _():
                z_copy(which, d, (z + ZED - d) % ZED, z).wait_recv()

        z_each(one)

    def finish(o, top):
        return o + jnp.where(lanes(o.shape) == 1, top, 0.0)

    all_entered()
    res_copy.start()
    for copy in w_out:
        copy.start()

    def early_wait(k, carry):
        h = (me + k) % GROUP
        remote(early_send.at[h], early.at[h], e_send.at[h], e_got.at[h], (base + h, tp)).wait_recv()
        return carry

    lax.fori_loop(1, GROUP, early_wait, 0)

    def place(j, carry):
        a = early[2 * j].astype(F32)
        b = early[2 * j + 1].astype(F32)

        def both(first, last):
            return jnp.concatenate([a[first:last], b[first:last]], axis=0).astype(BF16)

        k3[pl.ds(pl.multiple_of(z3 * 256 + j * 64, 64), 64)] = both(0, 32)
        k4[pl.ds(pl.multiple_of(z4 * 128 + j * 32, 32), 32)] = both(32, 48)
        k5[pl.ds(pl.multiple_of(z * 64 + j * 16, 16), 16)] = both(48, 56)
        return carry

    lax.fori_loop(0, GROUP // 2, place, 0)
    all_known()
    z_start()

    tri = lanes(square) <= sublanes(square)

    def causal_pair(q0, q1, kv0, kv1, v0, v1):
        s00 = jnp.where(tri, mmt(q0, kv0), MASKED)
        s10 = mmt(q1, kv0)
        s11 = jnp.where(tri, mmt(q1, kv1), MASKED)
        t0 = jnp.max(s00, axis=1, keepdims=True)
        t1 = jnp.max(jnp.maximum(s10, s11), axis=1, keepdims=True)
        p00 = jnp.exp2((s00 - t0) * EXPONENT).astype(BF16)
        p10 = jnp.exp2((s10 - t1) * EXPONENT).astype(BF16)
        p11 = jnp.exp2((s11 - t1) * EXPONENT).astype(BF16)
        return finish(mm(p00, v0), t0), finish(mm(p10, v0) + mm(p11, v1), t1)

    def near(m, carry):
        j = (y + (m % 3 + 1) * ((m + 3) // 4)) % 4

        def wait(s):
            remote(send.at[s], got.at[s], a_send.at[s], a_got.at[s], (base + s, tp)).wait_recv()

        wait_core = jnp.where(m == 0, 1 - core, 1)

        @pl.when(m > 0)
        def _():
            wait(2 * j)

        wait(2 * j + wait_core)
        kvs, qs, v1s, parts = [], [], [], []
        for i in range(2):
            kv = got[2 * j + i, 0:ROWS]
            packed = got[2 * j + i, ROWS : ROWS + 128].astype(F32)
            q = jnp.concatenate(
                [jnp.where(low_half, packed, 0.0), jnp.where(low_half, swap(packed), 0.0)], axis=0
            ).astype(BF16)
            kvs.append(kv)
            qs.append(q)
            v1s.append(with_ones(kv))
            parts.append((mm(choose[...], kv), mm(choose[...], q)))
        for i in range(2):
            kv, q = parts[i]
            pick_kv[j, 128 * i : 128 * i + 128] = kv[0:128].astype(BF16)
            pick_v1[j, 128 * i : 128 * i + 128] = with_ones(kv[0:128])
            pick_q[j, 128 * i : 128 * i + 128] = q[0:128].astype(BF16)

        def both(which, first, last):
            return jnp.concatenate([parts[0][which][first:last], parts[1][which][first:last]], axis=0)

        at = pl.ds(pl.multiple_of((j % 2) * 128, 128), 128)
        pick_kv[4 + j // 2, at] = both(0, 128, 192).astype(BF16)
        pick_v1[4 + j // 2, at] = with_ones(both(0, 128, 192))
        pick_q[4 + j // 2, at] = both(1, 128, 192).astype(BF16)
        far_q[pl.ds(pl.multiple_of(j * 64, 64), 64)] = both(1, 192, 224).astype(BF16)
        far_q[pl.ds(pl.multiple_of(256 + j * 32, 32), 32)] = both(1, 224, 240).astype(BF16)
        far_q[pl.ds(pl.multiple_of(384 + j * 16, 16), 16)] = both(1, 240, 248).astype(BF16)

        o0, o1 = causal_pair(qs[0], qs[1], kvs[0], kvs[1], v1s[0], v1s[1])
        near_out[2 * j] = o0
        near_out[2 * j + 1] = o1
        return carry

    lax.fori_loop(0, 4, near, 0)

    for copy in w_out:
        copy.wait_recv()
    w_on = [w_piece(w_first, 2, sibling, out_far), w_piece(w_second, 3, sibling, out_far)]
    for copy in w_on:
        copy.start()

    def picked(i):
        return causal_pair(
            pick_q[2 * i],
            pick_q[2 * i + 1],
            pick_kv[2 * i],
            pick_kv[2 * i + 1],
            pick_v1[2 * i],
            pick_v1[2 * i + 1],
        )

    for i in range(2):
        o0, o1 = picked(i)
        pick_out[4 * i, 0:128] = o0[0:128]
        pick_out[4 * i + 1, 0:128] = o0[128:256]
        pick_out[4 * i + 2, 0:128] = o1[0:128]
        pick_out[4 * i + 3, 0:128] = o1[128:256]
    o0, o1 = picked(2)
    for u in range(4):
        pick_out[u, 128:192] = o0[64 * u : 64 * u + 64]
        pick_out[4 + u, 128:192] = o1[64 * u : 64 * u + 64]

    z_finish_got()
    for buffer, q_first, count, slot, first in (
        (k3, 0, 256, z3, 192),
        (k4, 256, 128, z4, 224),
        (k5, 384, 64, z, 240),
    ):
        kv = buffer[...]
        q = far_q[q_first : q_first + count]
        shape = (count, 512)
        s = jnp.where(lanes(shape) <= sublanes(shape) + slot * count, mmt(q, kv), MASKED)
        t = jnp.max(s, axis=1, keepdims=True)
        p = jnp.exp2((s - t) * EXPONENT).astype(BF16)
        o = finish(mm(p, with_ones(kv)), t)
        each = count // GROUP
        for u in range(GROUP):
            pick_out[u, first : first + each] = o[each * u : each * u + each]

    tile = (ROWS, 128)
    lane = lanes(tile)
    branch = branch_of(sublanes(tile))
    mine = lane % 16 == branch
    covered = jnp.zeros(tile, jnp.int32)
    for b in range(1, 6):
        off = offsets[b, me] & (2**b - 1)
        hit = jnp.where(sublanes(tile) % 2**b == off, 1, 0)
        covered = jnp.where(lane % 16 == b, hit, covered)

    def split(x):
        high = x.astype(BF16)
        return high, (x - high.astype(F32)).astype(BF16)

    tops = jnp.zeros(tile, F32)
    bases = jnp.zeros(tile, F32)
    for s in range(GROUP):
        here = lane // 16 == s
        tops = jnp.where(here, pick_out[s, :, 1:2], tops)
        bases = jnp.where(here, near_out[s, :, 1:2], bases)
    first, rest = split(jnp.where(mine, tops, 0.0))
    second, third = split(jnp.where(mine, tops, 0.0) - first.astype(F32))
    spread = mm(choose_t[...], jnp.concatenate([first, second, third], axis=1))
    tops = spread[:, 0:128] + spread[:, 128:256] + spread[:, 256:384]
    tops = jnp.where(lane % 16 == 0, bases, jnp.where(covered == 1, tops, MASKED))
    top = tops
    for shift in (1, 2, 4):
        top = jnp.maximum(top, pltpu.roll(top, shift, 1))
    for shift in (127, 126, 124):
        top = jnp.maximum(top, pltpu.roll(top, shift, 1))
    share = jnp.exp2((tops - top) * EXPONENT)
    high, rest = split(share)
    back = mm(choose[...], jnp.concatenate([high, rest], axis=1))
    shares[0] = share
    shares[1] = jnp.where(mine, back[:, 0:128] + back[:, 128:256], 0.0)

    def mix_copy(to, r):
        return remote(
            mix_send.at[to, r],
            mix_own.at[me, r],
            m_send.at[2 * to + r],
            m_got.at[2 * me + r],
            (base + to, tp),
        )

    def mix_wait(h, r):
        remote(
            mix_send.at[h, r], mix_own.at[h, r], m_send.at[2 * h + r], m_got.at[2 * h + r], (base + h, tp)
        ).wait_recv()

    def far_copy(to, r):
        return remote(
            mix_send.at[to, r],
            mix_far.at[me, r],
            f_send.at[2 * to + r],
            f_got.at[2 * me + r],
            (base + to, 1 - tp),
        )

    def far_wait(h, r):
        remote(
            mix_send.at[h, r],
            mix_far.at[h, r],
            f_send.at[2 * h + r],
            f_got.at[2 * h + r],
            (base + h, 1 - tp),
        ).wait_recv()

    small = lanes((64, 128)) < 64

    for s in range(GROUP):
        mass = jnp.sum(jnp.where(lane // 16 == s, shares[1], 0.0), axis=1, keepdims=True)
        weighed[:, 128 * s : 128 * s + 128] = (pick_out[s] * mass).astype(BF16)

    for r in range(2):
        rows = slice(128 * r, 128 * r + 128)
        for pair in range(GROUP // 2):
            more = mm(choose_t[rows], weighed[:, 256 * pair : 256 * pair + 256])
            for c in range(2):
                s = 2 * pair + c
                both = near_out[s, rows] * shares[0, rows, 16 * s : 16 * s + 1]
                both = both + more[:, 128 * c : 128 * c + 128]
                mix = both / both[:, 0:1]
                mix_send[s, r] = jnp.where(small, swap(mix[0:64]), mix[64:128]).astype(BF16)

        def issue(i, carry):
            s = (me + i + 3) % GROUP
            far_copy(s, r).start()
            return carry

        def issue_own(i, carry):
            mix_copy((me + i) % GROUP, r).start()
            return carry

        lax.fori_loop(0, GROUP, issue, 0)
        lax.fori_loop(1, GROUP, issue_own, 0)
        mix_own[me, r] = mix_send[me, r]

    def widen(blocks, r):
        for pair in range(GROUP // 2):
            cut = slice(128 * pair, 128 * pair + 128)
            a = blocks[2 * pair, r].astype(F32)
            b = blocks[2 * pair + 1, r].astype(F32)
            mix_wide[r, 0:64, cut] = jnp.where(small, a, swap(b)).astype(BF16)
            mix_wide[r, 64:128, cut] = jnp.where(small, swap(a), b).astype(BF16)

    res_copy.wait_recv()
    for load in loads[6:]:
        load.wait()

    def near_hidden(r, carry):
        def own_wait(k, carry):
            mix_wait((me + k) % GROUP, r)
            return carry

        lax.fori_loop(1, GROUP, own_wait, 0)
        widen(mix_own, r)
        for n in range(4):
            cut = slice(256 * n, 256 * n + 256)
            rows = pl.ds(pl.multiple_of(128 * r, 128), 128)
            half_cut = slice(256 * (n % 2), 256 * (n % 2) + 256)
            hidden[r, :, cut] = mm(mix_wide[r], out_weight[:, cut]) + res_all[
                n // 2, rows, half_cut
            ].astype(F32)
        return carry

    lax.fori_loop(0, 2, near_hidden, 0)
    for copy in w_on:
        copy.wait_recv()
    for load in loads[0:3]:
        load.wait()

    def down_copy(r, n):
        return remote(
            down_send.at[r, n], down_got.at[r, n], d_send.at[2 * r + n], d_got.at[2 * r + n], partner
        )

    def feed(r, carry):
        def other_wait(h, carry):
            far_wait(h, r)
            return carry

        lax.fori_loop(0, GROUP, other_wait, 0)
        widen(mix_far, r)
        squares = jnp.zeros((128, 1), F32)
        for n in range(4):
            cut = slice(256 * n, 256 * n + 256)
            h = hidden[r, :, cut] + mm(mix_wide[r], out_far[:, cut])
            hidden[r, :, cut] = h
            squares = squares + jnp.sum(h * h, axis=1, keepdims=True)
        inverse = lax.rsqrt(squares / 1024.0 + 1e-5)
        for n in range(4):
            cut = slice(256 * n, 256 * n + 256)
            normed[r, :, cut] = (hidden[r, :, cut] * inverse * gain[:, cut]).astype(BF16)
        for n in range(4):
            cut = slice(256 * n, 256 * n + 256)
            gate = mm(normed[r], gate_w[:, cut])
            up = mm(normed[r], up_w[:, cut])
            act[r, :, cut] = (gate / (1.0 + jnp.exp(-gate)) * up).astype(BF16)
        for n in range(2):
            cut = pl.ds(pl.multiple_of((1 - tp) * COLS + n * 256, 256), 256)
            down_send[r, n] = mm(act[r], down_w[:, cut]).astype(BF16)
            down_copy(r, n).start()
        return carry

    lax.fori_loop(0, 2, feed, 0)

    def block_sent(k, carry):
        block_copy((me + k) % GROUP).wait_send()
        early_copy((me + k) % GROUP).wait_send()
        return carry

    lax.fori_loop(1, GROUP, block_sent, 0)
    for copy in w_out + w_on + [res_copy]:
        copy.wait_send()
    z_finish_send()

    def mix_sent(i, carry):
        for r in range(2):
            mix_copy((me + i) % GROUP, r).wait_send()
        return carry

    lax.fori_loop(1, GROUP, mix_sent, 0)

    def far_sent(h, carry):
        for r in range(2):
            far_copy(h, r).wait_send()
        return carry

    lax.fori_loop(0, GROUP, far_sent, 0)

    def last(r, carry):
        rows = pl.ds(pl.multiple_of(128 * r, 128), 128)
        for n in range(2):
            cut = pl.ds(pl.multiple_of(tp * COLS + n * 256, 256), 256)
            own = hidden[r, :, cut] + mm(act[r], down_w[:, cut])
            down_copy(r, n).wait_recv()
            out[rows, 256 * n : 256 * n + 256] = (own + down_got[r, n].astype(F32)).astype(BF16)
        return carry

    lax.fori_loop(0, 2, last, 0)

    for r in range(2):
        for n in range(2):
            down_copy(r, n).wait_send()


def shards(
    residual_in,
    queries,
    keys,
    values,
    head_offset,
    out_weight,
    norm_gain,
    gate_weight,
    up_weight,
    down_weight,
):
    vmem = pl.BlockSpec(memory_space=pltpu.VMEM)
    smem = pl.BlockSpec(memory_space=pltpu.SMEM)
    hbm = pl.BlockSpec(memory_space=pl.ANY)
    dma = pltpu.SemaphoreType.DMA
    scratch = [
        pltpu.VMEM((ROWS, COLS), BF16),
        pltpu.VMEM((ROWS, COLS), BF16),
        pltpu.VMEM((ROWS, COLS), BF16),
        pltpu.VMEM((1, 1024), F32),
        pltpu.VMEM((512, 1024), BF16),
        pltpu.VMEM((GROUP, 384, 128), BF16),
        pltpu.VMEM((GROUP, 384, 128), BF16),
        pltpu.VMEM((6, ROWS, 128), BF16),
        pltpu.VMEM((6, ROWS, 128), BF16),
        pltpu.VMEM((6, ROWS, 128), BF16),
        pltpu.VMEM((448, 128), BF16),
        pltpu.VMEM((512, 128), BF16),
        pltpu.VMEM((512, 128), BF16),
        pltpu.VMEM((512, 128), BF16),
        pltpu.VMEM((GROUP, ROWS, 128), F32),
        pltpu.VMEM((GROUP, ROWS, 128), F32),
        pltpu.VMEM((ROWS, ROWS), BF16),
        pltpu.VMEM((ROWS, ROWS), BF16),
        pltpu.VMEM((GROUP, 2, 64, 128), BF16),
        pltpu.VMEM((GROUP, 2, 64, 128), BF16),
        pltpu.VMEM((GROUP, 2, 64, 128), BF16),
        pltpu.VMEM((2, 128, COLS), BF16),
        pltpu.VMEM((2, ROWS, COLS), BF16),
        pltpu.VMEM((512, 1024), BF16),
        pltpu.VMEM((1024, 1024), BF16),
        pltpu.VMEM((1024, 1024), BF16),
        pltpu.VMEM((1024, 1024), BF16),
        pltpu.VMEM((2, 128, 1024), F32),
        pltpu.VMEM((2, 128, 1024), BF16),
        pltpu.VMEM((2, 128, 1024), BF16),
        pltpu.VMEM((2, 2, 128, 256), BF16),
        pltpu.VMEM((2, 2, 128, 256), BF16),
        pltpu.VMEM((2, ROWS, 128), F32),
        pltpu.VMEM((ROWS, GROUP * 128), BF16),
        dma((GROUP,)),
        dma((GROUP,)),
        dma((11,)),
        dma((11,)),
        dma((2 * GROUP,)),
        dma((2 * GROUP,)),
        dma((2 * GROUP,)),
        dma((2 * GROUP,)),
        dma((4,)),
        dma((4,)),
        dma,
        dma,
        dma((4,)),
        dma((4,)),
        dma((9,)),
        pltpu.SemaphoreType.REGULAR,
        pltpu.SemaphoreType.REGULAR,
        pltpu.VMEM((GROUP, 64, 128), BF16),
        pltpu.VMEM((GROUP, 64, 128), BF16),
        dma((GROUP,)),
        dma((GROUP,)),
    ]
    return pl.pallas_call(
        layer,
        out_shape=jax.ShapeDtypeStruct((ROWS, COLS), BF16),
        in_specs=[hbm, hbm, hbm, hbm, hbm, hbm, smem, hbm, hbm, hbm],
        out_specs=vmem,
        scratch_shapes=scratch,
        compiler_params=pltpu.CompilerParams(
            collective_id=0, has_side_effects=True, vmem_limit_bytes=60 * 2**20
        ),
        name="layer",
    )(
        queries,
        keys,
        values,
        residual_in,
        out_weight,
        norm_gain.reshape(1, 1024),
        head_offset,
        gate_weight,
        up_weight,
        down_weight,
    )


def solution(mesh):
    placed = (
        P("seq", "tp"),
        P("seq", "tp"),
        P("seq", "tp"),
        P("seq", "tp"),
        P(None, "tp"),
        P("tp", None),
        P(),
        P(None, "tp"),
        P(None, "tp"),
        P("tp", None),
    )
    return jax.shard_map(
        shards, mesh=mesh, in_specs=placed, out_specs=P("seq", "tp"), check_vma=False
    )
```

```python
import math

import jax
import jax.numpy as jnp
from jax import lax
from jax.experimental import pallas as pl
from jax.experimental.pallas import tpu as pltpu
from jax.sharding import PartitionSpec as P

MESH = pl.DeviceIdType.MESH
F32 = jnp.float32
BF16 = jnp.bfloat16

ROWS = 256
COLS = 512
GROUP = 8
ZED = 8
MASKED = -1e30
EXPONENT = math.log2(math.e) / 8.0


def lanes(shape):
    return lax.broadcasted_iota(jnp.int32, shape, len(shape) - 1)


def sublanes(shape):
    return lax.broadcasted_iota(jnp.int32, shape, 0)


def swap(x):
    return pltpu.roll(x, 64, 1)


def mm(a, b):
    return lax.dot_general(a, b, (((1,), (0,)), ((), ())), preferred_element_type=F32)


def mmt(a, b):
    return lax.dot_general(a, b, (((1,), (1,)), ((), ())), preferred_element_type=F32)


def with_ones(kv):
    lane = lanes(kv.shape)
    return jnp.where(lane < 64, jnp.where(lane == 0, 1.0, 0.0), kv.astype(F32)).astype(BF16)


def branch_of(i):
    one = jnp.where(i < 192, 2, jnp.where(i < 224, 3, jnp.where(i < 240, 4, jnp.where(i < 248, 5, 6))))
    return jnp.where(i < 128, 1, one)


def layer(
    q_hbm,
    k_hbm,
    v_hbm,
    res_hbm,
    out_hbm,
    gain_hbm,
    offsets,
    gate_hbm,
    up_hbm,
    down_hbm,
    out,
    queries,
    keys,
    values,
    gain,
    out_weight,
    send,
    got,
    pick_kv,
    pick_v1,
    pick_q,
    far_q,
    k3,
    k4,
    k5,
    near_out,
    pick_out,
    choose,
    choose_t,
    mix_send,
    mix_own,
    mix_far,
    mix_wide,
    res_all,
    out_far,
    gate_w,
    up_w,
    down_w,
    hidden,
    normed,
    act,
    down_send,
    down_got,
    shares,
    weighed,
    a_send,
    a_got,
    z_send,
    z_got,
    m_send,
    m_got,
    f_send,
    f_got,
    w_send,
    w_got,
    r_send,
    r_got,
    d_send,
    d_got,
    local,
    here_sem,
    all_sem,
    early_send,
    early,
    e_send,
    e_got,
):
    seq = lax.axis_index("seq")
    tp = lax.axis_index("tp")
    base = (seq // GROUP) * GROUP
    me = seq % GROUP
    y = me // 2
    core = me % 2
    z = (seq // GROUP) % ZED
    half = seq // (GROUP * ZED)
    plane = half * (GROUP * ZED)
    partner = (seq, 1 - tp)
    behind = ((1 - half) * (GROUP * ZED) + seq % (GROUP * ZED), 1 - tp)
    sibling = (base + me + 1 - 2 * core, tp)

    def remote(src, dst, s, r, to):
        return pltpu.make_async_remote_copy(
            src_ref=src, dst_ref=dst, send_sem=s, recv_sem=r, device_id=to, device_id_type=MESH
        )

    loads = [
        pltpu.make_async_copy(src, dst, local.at[i])
        for i, (src, dst) in enumerate(
            (
                (gate_hbm, gate_w),
                (up_hbm, up_w),
                (down_hbm, down_w),
                (k_hbm, keys),
                (v_hbm, values),
                (q_hbm, queries),
                (out_hbm, out_weight),
                (res_hbm, res_all.at[tp]),
                (gain_hbm, gain),
            )
        )
    ]
    for load in loads[3:6]:
        load.start()

    k3[...] = jnp.zeros_like(k3)
    k4[...] = jnp.zeros_like(k4)
    k5[...] = jnp.zeros_like(k5)
    barrier = pltpu.get_barrier_semaphore()
    lead = me == 0

    def greet(device):
        pl.semaphore_signal(barrier, inc=1, device_id=device, device_id_type=MESH)

    for k in range(1, GROUP):
        to = (me + k) % GROUP

        @pl.when(to != 0)
        def _():
            greet((base + to, tp))

    greet(partner)
    greet(behind)

    def group_entered():
        @pl.when(lead)
        def _():
            pl.semaphore_wait(here_sem, GROUP - 1)
            for d in range(1, ZED):
                greet((plane + ((z + d) % ZED) * GROUP, tp))

        @pl.when(me != 0)
        def _():
            pl.semaphore_wait(barrier, GROUP + 1)
            pl.semaphore_signal(here_sem, inc=1, device_id=(base, tp), device_id_type=MESH)

    def all_entered():
        @pl.when(lead)
        def _():
            pl.semaphore_wait(barrier, ZED + 1)
            for k in range(1, GROUP):
                pl.semaphore_signal(all_sem, inc=1, device_id=(base + k, tp), device_id_type=MESH)

    def all_known():
        @pl.when(me != 0)
        def _():
            pl.semaphore_wait(all_sem, 1)

    low = lanes((ROWS, 128)) < 64
    low_half = lanes((128, 128)) < 64

    def pack(pair):
        cut = pl.ds(pl.multiple_of(128 * pair, 128), 128)
        k = keys[:, cut].astype(F32)
        v = values[:, cut].astype(F32)
        q = queries[:, cut].astype(F32)
        send[2 * pair, 0:ROWS] = jnp.where(low, k, swap(v)).astype(BF16)
        send[2 * pair + 1, 0:ROWS] = jnp.where(low, swap(k), v).astype(BF16)
        top, bottom = q[0:128], q[128:256]
        send[2 * pair, ROWS : ROWS + 128] = jnp.where(low_half, top, swap(bottom)).astype(BF16)
        send[2 * pair + 1, ROWS : ROWS + 128] = jnp.where(low_half, swap(top), bottom).astype(BF16)

    def block_copy(to):
        return remote(send.at[to], got.at[me], a_send.at[to], a_got.at[me], (base + to, tp))

    def pick_early(head):
        wide = (64, ROWS)
        i = sublanes(wide)
        spot = jnp.full(wide, -1, jnp.int32)
        for b, first, count in ((3, 0, 32), (4, 32, 16), (5, 48, 8)):
            off = offsets[b, head] & (2**b - 1)
            spot = jnp.where((i >= first) & (i < first + count), (i - first) * 2**b + off, spot)
        rows = jnp.where(lanes(wide) == spot, 1.0, 0.0).astype(BF16)
        early_send[head] = mm(rows, send[head, 0:ROWS]).astype(BF16)

    def early_copy(to):
        return remote(early_send.at[to], early.at[me], e_send.at[to], e_got.at[me], (base + to, tp))

    def post(step, entered):
        pair = (y + step) % 4
        pack(pair)
        for c in range(2):
            pick_early(2 * pair + c)
        entered()
        for c in range(2):
            early_copy(2 * pair + c).start()
        for c in range(2):
            block_copy(2 * pair + c).start()

    for load in loads[3:6]:
        load.wait()
    post(2, group_entered)
    post(1, lambda: None)
    post(3, lambda: None)
    pack(y)
    for c in range(2):
        pick_early(2 * y + c)
    early_copy(me + 1 - 2 * core).start()
    a_last = block_copy(me + 1 - 2 * core)
    a_last.start()
    got[me] = send[me]
    early[me] = early_send[me]

    w_first = core * 128
    w_second = 256 + core * 128

    def w_piece(first, i, to, src):
        piece = pl.ds(pl.multiple_of(first, 128), 128)
        return remote(src.at[piece], out_far.at[piece], w_send.at[i], w_got.at[i], to)

    w_out = [w_piece(w_first, 0, partner, out_hbm), w_piece(w_second, 1, behind, out_hbm)]
    res_copy = remote(res_hbm, res_all.at[tp], r_send, r_got, partner)
    for load in loads[0:3] + loads[6:]:
        load.start()

    def target(i):
        spot = jnp.full(i.shape, -1, jnp.int32)
        first = 0
        for b in range(1, 6):
            rate = 2**b
            count = ROWS // rate
            off = offsets[b, me] & (rate - 1)
            inside = (i >= first) & (i < first + count)
            spot = jnp.where(inside, (i - first) * rate + off, spot)
            first += count
        return spot

    square = (ROWS, ROWS)
    choose[...] = jnp.where(lanes(square) == target(sublanes(square)), 1.0, 0.0).astype(BF16)
    choose_t[...] = jnp.where(sublanes(square) == target(lanes(square)), 1.0, 0.0).astype(BF16)
    pick_out[:, 248:256] = jnp.zeros((GROUP, 8, 128), F32)

    z3 = z % 2
    z4 = z % 4

    def z_copy(which, d, sender, to):
        buffer, count, slot, at = (
            (k3, 256, sender % 2, 0),
            (k4, 128, sender % 4, d),
            (k5, 64, sender, 3 + d),
        )[which]
        piece = buffer.at[pl.ds(pl.multiple_of(slot * count, 64), count)]
        return remote(piece, piece, z_send.at[at], z_got.at[at], (plane + to * GROUP + me, tp))

    def z_each(act_on):
        for d in range(ZED - 1, 0, -1):
            if d == 1:
                act_on(0, d, z3)
            if d < 4:
                act_on(1, d, z4)
            act_on(2, d, z)

    def z_start():
        sizes = (2, 4, 8)

        def one(which, d, slot):
            @pl.when(slot + d < sizes[which])
            def _():
                z_copy(which, d, z, (z + d) % ZED).start()

        z_each(one)

    def z_finish_send():
        sizes = (2, 4, 8)

        def one(which, d, slot):
            @pl.when(slot + d < sizes[which])
            def _():
                z_copy(which, d, z, (z + d) % ZED).wait_send()

        z_each(one)

    def z_finish_got():
        def one(which, d, slot):
            @pl.when(slot >= d)
            def _():
                z_copy(which, d, (z + ZED - d) % ZED, z).wait_recv()

        z_each(one)

    def finish(o, top):
        return o + jnp.where(lanes(o.shape) == 1, top, 0.0)

    all_entered()
    res_copy.start()
    for copy in w_out:
        copy.start()

    def early_wait(k, carry):
        h = (me + k) % GROUP
        remote(early_send.at[h], early.at[h], e_send.at[h], e_got.at[h], (base + h, tp)).wait_recv()
        return carry

    lax.fori_loop(1, GROUP, early_wait, 0)

    def place(j, carry):
        a = early[2 * j].astype(F32)
        b = early[2 * j + 1].astype(F32)

        def both(first, last):
            return jnp.concatenate([a[first:last], b[first:last]], axis=0).astype(BF16)

        k3[pl.ds(pl.multiple_of(z3 * 256 + j * 64, 64), 64)] = both(0, 32)
        k4[pl.ds(pl.multiple_of(z4 * 128 + j * 32, 32), 32)] = both(32, 48)
        k5[pl.ds(pl.multiple_of(z * 64 + j * 16, 16), 16)] = both(48, 56)
        return carry

    for j in range(GROUP // 2):
        place(j, 0)
    all_known()
    z_start()

    tri = lanes(square) <= sublanes(square)

    def causal_pair(q0, q1, kv0, kv1, v0, v1):
        s00 = jnp.where(tri, mmt(q0, kv0), MASKED)
        s10 = mmt(q1, kv0)
        s11 = jnp.where(tri, mmt(q1, kv1), MASKED)
        t0 = jnp.max(s00, axis=1, keepdims=True)
        t1 = jnp.max(jnp.maximum(s10, s11), axis=1, keepdims=True)
        p00 = jnp.exp2((s00 - t0) * EXPONENT).astype(BF16)
        p10 = jnp.exp2((s10 - t1) * EXPONENT).astype(BF16)
        p11 = jnp.exp2((s11 - t1) * EXPONENT).astype(BF16)
        return finish(mm(p00, v0), t0), finish(mm(p10, v0) + mm(p11, v1), t1)

    def near(m, carry):
        j = (y + (m % 3 + 1) * ((m + 3) // 4)) % 4

        def wait(s):
            remote(send.at[s], got.at[s], a_send.at[s], a_got.at[s], (base + s, tp)).wait_recv()

        wait_core = jnp.where(m == 0, 1 - core, 1)

        @pl.when(m > 0)
        def _():
            wait(2 * j)

        wait(2 * j + wait_core)
        kvs, qs, v1s, parts = [], [], [], []
        for i in range(2):
            kv = got[2 * j + i, 0:ROWS]
            packed = got[2 * j + i, ROWS : ROWS + 128].astype(F32)
            q = jnp.concatenate(
                [jnp.where(low_half, packed, 0.0), jnp.where(low_half, swap(packed), 0.0)], axis=0
            ).astype(BF16)
            kvs.append(kv)
            qs.append(q)
            v1s.append(with_ones(kv))
            parts.append((mm(choose[...], kv), mm(choose[...], q)))
        for i in range(2):
            kv, q = parts[i]
            pick_kv[j, 128 * i : 128 * i + 128] = kv[0:128].astype(BF16)
            pick_v1[j, 128 * i : 128 * i + 128] = with_ones(kv[0:128])
            pick_q[j, 128 * i : 128 * i + 128] = q[0:128].astype(BF16)

        def both(which, first, last):
            return jnp.concatenate([parts[0][which][first:last], parts[1][which][first:last]], axis=0)

        at = pl.ds(pl.multiple_of((j % 2) * 128, 128), 128)
        pick_kv[4 + j // 2, at] = both(0, 128, 192).astype(BF16)
        pick_v1[4 + j // 2, at] = with_ones(both(0, 128, 192))
        pick_q[4 + j // 2, at] = both(1, 128, 192).astype(BF16)
        far_q[pl.ds(pl.multiple_of(j * 64, 64), 64)] = both(1, 192, 224).astype(BF16)
        far_q[pl.ds(pl.multiple_of(256 + j * 32, 32), 32)] = both(1, 224, 240).astype(BF16)
        far_q[pl.ds(pl.multiple_of(384 + j * 16, 16), 16)] = both(1, 240, 248).astype(BF16)

        o0, o1 = causal_pair(qs[0], qs[1], kvs[0], kvs[1], v1s[0], v1s[1])
        near_out[2 * j] = o0
        near_out[2 * j + 1] = o1
        return carry

    lax.fori_loop(0, 4, near, 0)

    for copy in w_out:
        copy.wait_recv()
    w_on = [w_piece(w_first, 2, sibling, out_far), w_piece(w_second, 3, sibling, out_far)]
    for copy in w_on:
        copy.start()

    def picked(i):
        return causal_pair(
            pick_q[2 * i],
            pick_q[2 * i + 1],
            pick_kv[2 * i],
            pick_kv[2 * i + 1],
            pick_v1[2 * i],
            pick_v1[2 * i + 1],
        )

    for i in range(2):
        o0, o1 = picked(i)
        pick_out[4 * i, 0:128] = o0[0:128]
        pick_out[4 * i + 1, 0:128] = o0[128:256]
        pick_out[4 * i + 2, 0:128] = o1[0:128]
        pick_out[4 * i + 3, 0:128] = o1[128:256]
    o0, o1 = picked(2)
    for u in range(4):
        pick_out[u, 128:192] = o0[64 * u : 64 * u + 64]
        pick_out[4 + u, 128:192] = o1[64 * u : 64 * u + 64]

    z_finish_got()
    for buffer, q_first, count, slot, first in (
        (k3, 0, 256, z3, 192),
        (k4, 256, 128, z4, 224),
        (k5, 384, 64, z, 240),
    ):
        kv = buffer[...]
        q = far_q[q_first : q_first + count]
        shape = (count, 512)
        s = jnp.where(lanes(shape) <= sublanes(shape) + slot * count, mmt(q, kv), MASKED)
        t = jnp.max(s, axis=1, keepdims=True)
        p = jnp.exp2((s - t) * EXPONENT).astype(BF16)
        o = finish(mm(p, with_ones(kv)), t)
        each = count // GROUP
        for u in range(GROUP):
            pick_out[u, first : first + each] = o[each * u : each * u + each]

    tile = (ROWS, 128)
    lane = lanes(tile)
    branch = branch_of(sublanes(tile))
    mine = lane % 16 == branch
    covered = jnp.zeros(tile, jnp.int32)
    for b in range(1, 6):
        off = offsets[b, me] & (2**b - 1)
        hit = jnp.where(sublanes(tile) % 2**b == off, 1, 0)
        covered = jnp.where(lane % 16 == b, hit, covered)

    def split(x):
        high = x.astype(BF16)
        return high, (x - high.astype(F32)).astype(BF16)

    tops = jnp.zeros(tile, F32)
    bases = jnp.zeros(tile, F32)
    for s in range(GROUP):
        here = lane // 16 == s
        tops = jnp.where(here, pick_out[s, :, 1:2], tops)
        bases = jnp.where(here, near_out[s, :, 1:2], bases)
    first, rest = split(jnp.where(mine, tops, 0.0))
    second, third = split(jnp.where(mine, tops, 0.0) - first.astype(F32))
    spread = mm(choose_t[...], jnp.concatenate([first, second, third], axis=1))
    tops = spread[:, 0:128] + spread[:, 128:256] + spread[:, 256:384]
    tops = jnp.where(lane % 16 == 0, bases, jnp.where(covered == 1, tops, MASKED))
    top = tops
    for shift in (1, 2, 4):
        top = jnp.maximum(top, pltpu.roll(top, shift, 1))
    for shift in (127, 126, 124):
        top = jnp.maximum(top, pltpu.roll(top, shift, 1))
    share = jnp.exp2((tops - top) * EXPONENT)
    high, rest = split(share)
    back = mm(choose[...], jnp.concatenate([high, rest], axis=1))
    shares[0] = share
    shares[1] = jnp.where(mine, back[:, 0:128] + back[:, 128:256], 0.0)

    def mix_copy(to, r):
        return remote(
            mix_send.at[to, r],
            mix_own.at[me, r],
            m_send.at[2 * to + r],
            m_got.at[2 * me + r],
            (base + to, tp),
        )

    def mix_wait(h, r):
        remote(
            mix_send.at[h, r], mix_own.at[h, r], m_send.at[2 * h + r], m_got.at[2 * h + r], (base + h, tp)
        ).wait_recv()

    def far_copy(to, r):
        return remote(
            mix_send.at[to, r],
            mix_far.at[me, r],
            f_send.at[2 * to + r],
            f_got.at[2 * me + r],
            (base + to, 1 - tp),
        )

    def far_wait(h, r):
        remote(
            mix_send.at[h, r],
            mix_far.at[h, r],
            f_send.at[2 * h + r],
            f_got.at[2 * h + r],
            (base + h, 1 - tp),
        ).wait_recv()

    small = lanes((64, 128)) < 64

    for s in range(GROUP):
        mass = jnp.sum(jnp.where(lane // 16 == s, shares[1], 0.0), axis=1, keepdims=True)
        weighed[:, 128 * s : 128 * s + 128] = (pick_out[s] * mass).astype(BF16)

    for r in range(2):
        rows = slice(128 * r, 128 * r + 128)
        for pair in range(GROUP // 2):
            more = mm(choose_t[rows], weighed[:, 256 * pair : 256 * pair + 256])
            for c in range(2):
                s = 2 * pair + c
                both = near_out[s, rows] * shares[0, rows, 16 * s : 16 * s + 1]
                both = both + more[:, 128 * c : 128 * c + 128]
                mix = both / both[:, 0:1]
                mix_send[s, r] = jnp.where(small, swap(mix[0:64]), mix[64:128]).astype(BF16)

        def issue(i, carry):
            s = (me + i + 3) % GROUP
            far_copy(s, r).start()
            return carry

        def issue_own(i, carry):
            mix_copy((me + i) % GROUP, r).start()
            return carry

        lax.fori_loop(0, GROUP, issue, 0)
        lax.fori_loop(1, GROUP, issue_own, 0)
        mix_own[me, r] = mix_send[me, r]

    def widen(blocks, r):
        for pair in range(GROUP // 2):
            cut = slice(128 * pair, 128 * pair + 128)
            a = blocks[2 * pair, r].astype(F32)
            b = blocks[2 * pair + 1, r].astype(F32)
            mix_wide[r, 0:64, cut] = jnp.where(small, a, swap(b)).astype(BF16)
            mix_wide[r, 64:128, cut] = jnp.where(small, swap(a), b).astype(BF16)

    res_copy.wait_recv()
    for load in loads[6:]:
        load.wait()

    def near_hidden(r, carry):
        def own_wait(k, carry):
            mix_wait((me + k) % GROUP, r)
            return carry

        lax.fori_loop(1, GROUP, own_wait, 0)
        widen(mix_own, r)
        for n in range(4):
            cut = slice(256 * n, 256 * n + 256)
            rows = pl.ds(pl.multiple_of(128 * r, 128), 128)
            half_cut = slice(256 * (n % 2), 256 * (n % 2) + 256)
            hidden[r, :, cut] = mm(mix_wide[r], out_weight[:, cut]) + res_all[
                n // 2, rows, half_cut
            ].astype(F32)
        return carry

    lax.fori_loop(0, 2, near_hidden, 0)
    for copy in w_on:
        copy.wait_recv()
    for load in loads[0:3]:
        load.wait()

    def down_copy(r, n):
        return remote(
            down_send.at[r, n], down_got.at[r, n], d_send.at[2 * r + n], d_got.at[2 * r + n], partner
        )

    def feed(r, carry):
        def other_wait(h, carry):
            far_wait(h, r)
            return carry

        lax.fori_loop(0, GROUP, other_wait, 0)
        widen(mix_far, r)
        squares = jnp.zeros((128, 1), F32)
        for n in range(4):
            cut = slice(256 * n, 256 * n + 256)
            h = hidden[r, :, cut] + mm(mix_wide[r], out_far[:, cut])
            hidden[r, :, cut] = h
            squares = squares + jnp.sum(h * h, axis=1, keepdims=True)
        inverse = lax.rsqrt(squares / 1024.0 + 1e-5)
        for n in range(4):
            cut = slice(256 * n, 256 * n + 256)
            normed[r, :, cut] = (hidden[r, :, cut] * inverse * gain[:, cut]).astype(BF16)
        for n in range(4):
            cut = slice(256 * n, 256 * n + 256)
            gate = mm(normed[r], gate_w[:, cut])
            up = mm(normed[r], up_w[:, cut])
            act[r, :, cut] = (gate / (1.0 + jnp.exp(-gate)) * up).astype(BF16)
        for n in range(2):
            cut = pl.ds(pl.multiple_of((1 - tp) * COLS + n * 256, 256), 256)
            down_send[r, n] = mm(act[r], down_w[:, cut]).astype(BF16)
            down_copy(r, n).start()
        return carry

    lax.fori_loop(0, 2, feed, 0)

    def block_sent(k, carry):
        block_copy((me + k) % GROUP).wait_send()
        early_copy((me + k) % GROUP).wait_send()
        return carry

    lax.fori_loop(1, GROUP, block_sent, 0)
    for copy in w_out + w_on + [res_copy]:
        copy.wait_send()
    z_finish_send()

    def mix_sent(i, carry):
        for r in range(2):
            mix_copy((me + i) % GROUP, r).wait_send()
        return carry

    lax.fori_loop(1, GROUP, mix_sent, 0)

    def far_sent(h, carry):
        for r in range(2):
            far_copy(h, r).wait_send()
        return carry

    lax.fori_loop(0, GROUP, far_sent, 0)

    def last(r, carry):
        rows = pl.ds(pl.multiple_of(128 * r, 128), 128)
        for n in range(2):
            cut = pl.ds(pl.multiple_of(tp * COLS + n * 256, 256), 256)
            own = hidden[r, :, cut] + mm(act[r], down_w[:, cut])
            down_copy(r, n).wait_recv()
            out[rows, 256 * n : 256 * n + 256] = (own + down_got[r, n].astype(F32)).astype(BF16)
        return carry

    lax.fori_loop(0, 2, last, 0)

    for r in range(2):
        for n in range(2):
            down_copy(r, n).wait_send()


def shards(
    residual_in,
    queries,
    keys,
    values,
    head_offset,
    out_weight,
    norm_gain,
    gate_weight,
    up_weight,
    down_weight,
):
    vmem = pl.BlockSpec(memory_space=pltpu.VMEM)
    smem = pl.BlockSpec(memory_space=pltpu.SMEM)
    hbm = pl.BlockSpec(memory_space=pl.ANY)
    dma = pltpu.SemaphoreType.DMA
    scratch = [
        pltpu.VMEM((ROWS, COLS), BF16),
        pltpu.VMEM((ROWS, COLS), BF16),
        pltpu.VMEM((ROWS, COLS), BF16),
        pltpu.VMEM((1, 1024), F32),
        pltpu.VMEM((512, 1024), BF16),
        pltpu.VMEM((GROUP, 384, 128), BF16),
        pltpu.VMEM((GROUP, 384, 128), BF16),
        pltpu.VMEM((6, ROWS, 128), BF16),
        pltpu.VMEM((6, ROWS, 128), BF16),
        pltpu.VMEM((6, ROWS, 128), BF16),
        pltpu.VMEM((448, 128), BF16),
        pltpu.VMEM((512, 128), BF16),
        pltpu.VMEM((512, 128), BF16),
        pltpu.VMEM((512, 128), BF16),
        pltpu.VMEM((GROUP, ROWS, 128), F32),
        pltpu.VMEM((GROUP, ROWS, 128), F32),
        pltpu.VMEM((ROWS, ROWS), BF16),
        pltpu.VMEM((ROWS, ROWS), BF16),
        pltpu.VMEM((GROUP, 2, 64, 128), BF16),
        pltpu.VMEM((GROUP, 2, 64, 128), BF16),
        pltpu.VMEM((GROUP, 2, 64, 128), BF16),
        pltpu.VMEM((2, 128, COLS), BF16),
        pltpu.VMEM((2, ROWS, COLS), BF16),
        pltpu.VMEM((512, 1024), BF16),
        pltpu.VMEM((1024, 1024), BF16),
        pltpu.VMEM((1024, 1024), BF16),
        pltpu.VMEM((1024, 1024), BF16),
        pltpu.VMEM((2, 128, 1024), F32),
        pltpu.VMEM((2, 128, 1024), BF16),
        pltpu.VMEM((2, 128, 1024), BF16),
        pltpu.VMEM((2, 2, 128, 256), BF16),
        pltpu.VMEM((2, 2, 128, 256), BF16),
        pltpu.VMEM((2, ROWS, 128), F32),
        pltpu.VMEM((ROWS, GROUP * 128), BF16),
        dma((GROUP,)),
        dma((GROUP,)),
        dma((11,)),
        dma((11,)),
        dma((2 * GROUP,)),
        dma((2 * GROUP,)),
        dma((2 * GROUP,)),
        dma((2 * GROUP,)),
        dma((4,)),
        dma((4,)),
        dma,
        dma,
        dma((4,)),
        dma((4,)),
        dma((9,)),
        pltpu.SemaphoreType.REGULAR,
        pltpu.SemaphoreType.REGULAR,
        pltpu.VMEM((GROUP, 64, 128), BF16),
        pltpu.VMEM((GROUP, 64, 128), BF16),
        dma((GROUP,)),
        dma((GROUP,)),
    ]
    return pl.pallas_call(
        layer,
        out_shape=jax.ShapeDtypeStruct((ROWS, COLS), BF16),
        in_specs=[hbm, hbm, hbm, hbm, hbm, hbm, smem, hbm, hbm, hbm],
        out_specs=vmem,
        scratch_shapes=scratch,
        compiler_params=pltpu.CompilerParams(
            collective_id=0, has_side_effects=True, vmem_limit_bytes=60 * 2**20
        ),
        name="layer",
    )(
        queries,
        keys,
        values,
        residual_in,
        out_weight,
        norm_gain.reshape(1, 1024),
        head_offset,
        gate_weight,
        up_weight,
        down_weight,
    )


def solution(mesh):
    placed = (
        P("seq", "tp"),
        P("seq", "tp"),
        P("seq", "tp"),
        P("seq", "tp"),
        P(None, "tp"),
        P("tp", None),
        P(),
        P(None, "tp"),
        P(None, "tp"),
        P("tp", None),
    )
    return jax.shard_map(
        shards, mesh=mesh, in_specs=placed, out_specs=P("seq", "tp"), check_vma=False
    )
```
